32 devices in a mesh: group: 2 (over y), adapter: 8 (over z, core), tensor: 2 (over x), sub: 1.
Axes of the slice: x: 2, y: 2, z: 4, core: 2. Of those that a mesh axis runs over, the one named last changes fastest.
Arguments:
- tokens: bfloat16 [4096, 8192], P(('group', 'adapter'), ('tensor', 'sub')), parts along dimension 0, may hold values from -6 to 6
- token_adapter_index: int32 [4096], P(('group', 'adapter')), parts along dimension 0, may hold values from 0 to 63, as said below
- table: int32 [128], P('group'), parts along dimension 0, may hold values from 0 to 63, as said below
- value_matrix: bfloat16 [8192, 1024], P(('tensor', 'sub')), may hold values from -0.0625 to 0.0625
- shrink_weight: float32 [8192, 1024], P(('tensor', 'sub'), 'adapter'), may hold values from -0.0625 to 0.0625
- expand_weight: float32 [64, 16, 1024], P('adapter', None, ('tensor', 'sub')), may hold values from -1.5 to 1.5
Outputs:
- values: bfloat16 [4096, 1024], P(('group', 'adapter'), ('tensor', 'sub')), parts along dimension 0
The draws below stay inside these ranges and needn't reach their ends.
There are 2 independent parts, one for each index of `group`. The reference program is written for one: setup_inputs(seed, part) draws one part's arguments, and reference() takes and returns one part's arrays. A program takes and returns all parts, laid end to end along the dimension named above; an argument that names none is the same for every part. Nothing has to cross between parts.
Inputs may be any that keep to these rules, and one draw needn't show every extreme that they name: A permutation: adapter a sits in slot table[a], which index table[a] // 8 of the adapter axis holds. `token_adapter_index`: among the 256 tokens of one index of the adapter axis, at most 128 use adapters held by any one index.
All inputs are finite; a program needn't handle non-finite values.
Results may differ from the reference program's by a relative error of at most 0.00115.
Values may be sent and summed in bfloat16 or wider, within the bound.
No kernel may reach another device: no remote copies, remote signals or barrier semaphores. Data moves between devices by JAX's collectives and lax.ppermute only.
A program may use at most 64 MiB of HBM per device.

```python
import math
import jax
import jax.numpy as jnp
from jax import lax

MODEL_WIDTH = 8192
VALUE_FEATURES = 1024
ADAPTER_RANK = 16
ADP_DEV = 8
TOK_DEV = 256
ADAPTER_COUNT = 64
STEP_TOKENS = 2048
CAP = 128
N_ADAPTER = 8


def placement_order(key):
    return jax.random.permutation(key, ADAPTER_COUNT).astype(jnp.int32)


def draw_table(key, part):
    order = placement_order(key)
    return order


def draw_token_adapter_index(key, part):
    order = placement_order(key)
    key = jax.random.fold_in(key, 7)
    at_slot = jnp.argsort(order).astype(jnp.int32)
    hot_key, block_key = jax.random.split(key)
    hot_owner = jax.random.randint(hot_key, (), 0, N_ADAPTER)
    spare_rows = TOK_DEV - CAP
    least_spread = max(1, -(-spare_rows // CAP))

    def single_block(block_seed):
        key_others, key_spread, key_local, key_order = jax.random.split(block_seed, 4)
        others = (hot_owner + 1 + jax.random.permutation(key_others, N_ADAPTER - 1)) % N_ADAPTER
        spread = jax.random.randint(key_spread, (), least_spread, N_ADAPTER)
        position = jnp.arange(TOK_DEV, dtype=jnp.int32)
        owner_index = jnp.where(position < CAP, hot_owner, others[(position - CAP) % spread])
        held_index = jax.random.randint(key_local, (TOK_DEV,), 0, ADP_DEV)
        chosen = at_slot[owner_index * ADP_DEV + held_index]
        return chosen[jax.random.permutation(key_order, TOK_DEV)]
    block_keys = jax.random.split(block_key, N_ADAPTER)
    return jax.vmap(single_block)(block_keys).reshape(-1).astype(jnp.int32)


def level_of(own_key, shape, shards, low, largest):
    gain, own = 1.0, jax.random.fold_in(own_key, 6)
    for dim, parts in shards:
        steps = jnp.exp(jax.random.uniform(jax.random.fold_in(own, dim), (parts,), jnp.float32, low / len(shards), largest / len(shards)))
        gain = gain * jnp.repeat(steps, shape[dim] // parts).reshape([-1 if axis == dim else 1 for axis in range(len(shape))])
    return gain


def normal_values(rng, shape, scale, reach, shards=(), kind=jnp.bfloat16):
    result = scale * jax.random.normal(rng, shape, jnp.float32)
    if shards:
        result = result * level_of(rng, shape, shards, -0.22, 0.18)
    return jnp.clip(result, -reach, reach).astype(kind)


def setup_inputs(seed: int = 0, part: int = 0) -> dict:
    seeds = jax.random.split(jax.random.key(seed), 7)
    part_keys = jax.random.split(jax.random.fold_in(seeds[6], part), 7)
    return {
        "tokens": normal_values(part_keys[0], (STEP_TOKENS, MODEL_WIDTH), 1.0, 6.0, ((0, 8), (1, 2))),
        "token_adapter_index": draw_token_adapter_index(jax.random.fold_in(jax.random.fold_in(seeds[6], part), 71), part),
        "table": draw_table(jax.random.fold_in(jax.random.fold_in(seeds[6], part), 71), part),
        "value_matrix": normal_values(seeds[3], (MODEL_WIDTH, VALUE_FEATURES), MODEL_WIDTH ** -0.5, 0.0625, ((0, 2),)),
        "shrink_weight": normal_values(seeds[4], (MODEL_WIDTH, ADAPTER_COUNT * ADAPTER_RANK), MODEL_WIDTH ** -0.5, 0.0625, ((0, 2), (1, 8)), jnp.float32),
        "expand_weight": normal_values(seeds[5], (ADAPTER_COUNT, ADAPTER_RANK, VALUE_FEATURES), ADAPTER_RANK ** -0.5, 1.5, ((0, 8), (2, 2)), jnp.float32),
    }


SCALING = 0.5


def reference(tokens, token_adapter_index, table, value_matrix, shrink_weight, expand_weight):
    slot_number = table[token_adapter_index].astype(jnp.int32)
    base_output = jnp.dot(tokens, value_matrix, preferred_element_type=jnp.float32)
    shrink_every_slot = shrink_weight.reshape(MODEL_WIDTH, ADAPTER_COUNT, ADAPTER_RANK)
    block_length = math.gcd(STEP_TOKENS, 128)

    def single_block(fragments):
        row_block, slot_columns = fragments
        selected = jnp.take(shrink_every_slot, slot_columns, axis=1)
        shrunk = jnp.einsum("td,dtr->tr", row_block.astype(jnp.float32), selected, precision=lax.Precision.HIGHEST)
        expand_matrix = jnp.take(expand_weight, slot_columns, axis=0)
        return SCALING * jnp.einsum("tr,trk->tk", shrunk, expand_matrix, precision=lax.Precision.HIGHEST)

    adapter_update = lax.map(single_block, (tokens.reshape(-1, block_length, MODEL_WIDTH), slot_number.reshape(-1, block_length)))
    adapter_update = adapter_update.reshape(STEP_TOKENS, VALUE_FEATURES)
    return (base_output + adapter_update).astype(jnp.bfloat16)
```

```python
import jax
import jax.numpy as jnp
from jax import lax
from jax.sharding import PartitionSpec as P

SCALING = 0.5
SHRINK_GAIN = 2.0**19
EXPAND_GAIN = 2.0**14


def chain(piece, half, spots):
    def shift(value, step, senders):
        pairs = [(2 * s + c, 2 * (s + step) + c) for s in senders for c in range(2)]
        return lax.ppermute(value, "adapter", pairs)

    found = [(piece, half)]
    up = down = piece
    merged = None
    for step in range(1, spots):
        goes_up = list(range(step - 1, spots - 1))
        goes_down = list(range(1, spots - step + 1))
        source = jnp.where(half >= step, half - step, half + step)
        valid = (half >= step) | (half + step < spots)
        if 2 * step - 1 > spots:
            pairs = [(2 * s + c, 2 * (s + 1) + c) for s in goes_up for c in range(2)]
            pairs += [(2 * s + c, 2 * (s - 1) + c) for s in goes_down for c in range(2)]
            merged = lax.ppermute(merged, "adapter", pairs)
        else:
            up, down = shift(up, 1, goes_up), shift(down, -1, goes_down)
            if 2 * step > spots - 1:
                merged = jnp.where(half >= step, up, down)
            else:
                found.append((up, jnp.where(half >= step, half - step, -1)))
                found.append((down, jnp.where(half + step < spots, half + step, -1)))
                continue
        found.append((merged, jnp.where(valid, source, -1)))
    return found


def two_terms(value):
    wide = value.astype(jnp.float32)
    high = lax.reduce_precision(wide, exponent_bits=8, mantissa_bits=7)
    return high.astype(jnp.bfloat16), (wide - high).astype(jnp.bfloat16)


def per_device(tokens, token_adapter_index, table, value_matrix, shrink_weight, expand_weight):
    rows, width = tokens.shape
    resident, rank, span = expand_weight.shape
    held = resident * rank
    owners = lax.axis_size("adapter")
    spots = owners // 2
    quarter = width // 4
    g, a = lax.axis_index("group"), lax.axis_index("adapter")
    c, half = a % 2, a // 2
    core_pairs = [(i, i ^ 1) for i in range(owners)]
    swap = [(0, 1), (1, 0)]

    def over_core(value):
        return lax.ppermute(value, "adapter", core_pairs)

    def over_group(value):
        return lax.ppermute(value, "group", swap)

    flat_expand = expand_weight.reshape(held, span)

    def encoded(side):
        place = 2 * side + g
        shrink = lax.dynamic_slice_in_dim(shrink_weight, place * quarter, quarter, 0)
        expand = lax.dynamic_slice_in_dim(flat_expand, place * (span // 4), span // 4, 1)
        return jnp.concatenate(
            [
                (shrink * SHRINK_GAIN).astype(jnp.float16),
                (expand * EXPAND_GAIN).astype(jnp.float16).reshape(-1, held),
            ],
            axis=0,
        )

    given = over_core(encoded(1 - c))
    mine = encoded(c)
    chains = [(chain(mine, half, spots), c), (chain(given, half, spots), 1 - c)]

    matches = token_adapter_index[:, None] == lax.broadcasted_iota(
        jnp.int32, (rows, table.shape[0]), 1
    )
    slot = jnp.sum(jnp.where(matches, table[None, :], 0), axis=1)
    keep = lax.dynamic_slice_in_dim(tokens, c * 2 * quarter, 2 * quarter, 1)
    give = lax.dynamic_slice_in_dim(tokens, (1 - c) * 2 * quarter, 2 * quarter, 1)
    pair = jnp.concatenate([keep, over_core(give)], axis=0)
    pair_slot = jnp.concatenate([slot, over_core(slot)])
    own_part = lax.dynamic_slice_in_dim(pair, g * quarter, quarter, 1)
    other_part = lax.dynamic_slice_in_dim(pair, (1 - g) * quarter, quarter, 1)
    every = jnp.concatenate([own_part, over_group(other_part)], axis=0)
    every_slot = jnp.concatenate([pair_slot, over_group(pair_slot)])

    partial = jnp.dot(tokens, value_matrix, preferred_element_type=jnp.float32)
    axes = ("tensor", "sub")
    two = lax.axis_size("tensor") == 2 and lax.axis_size("sub") == 1
    if two:
        x = lax.axis_index("tensor")
        sent = lax.dynamic_slice_in_dim(partial, (1 - x) * span, span, 1)
        base = lax.dynamic_slice_in_dim(partial, x * span, span, 1) + lax.ppermute(
            sent, "tensor", swap
        )
    else:
        base = lax.psum_scatter(partial, axes, scatter_dimension=1, tiled=True)

    lane_slot = lax.broadcasted_iota(jnp.int32, (1, held), 1) // rank
    total = jnp.zeros((every.shape[0], held), jnp.float32)
    for pieces, side in chains:
        for piece, source in pieces:
            high, low = two_terms(piece[:quarter])
            product = jnp.dot(
                every, jnp.concatenate([high, low], axis=1), preferred_element_type=jnp.float32
            )
            first = jnp.where(source < 0, -(2**20), (2 * source + side) * resident)
            total = jnp.where(
                every_slot[:, None] == lane_slot + first,
                product[:, :held] + product[:, held:],
                total,
            )
    compact = jnp.sum(total.reshape(-1, resident, rank), axis=1)
    compact = jnp.transpose(compact)
    pair_sum = compact[:, : 2 * rows] + over_group(compact[:, 2 * rows :])
    own_sum = pair_sum[:, :rows] + over_core(pair_sum[:, rows:])
    if two:
        own_sum = own_sum + lax.ppermute(own_sum, "tensor", swap)
    else:
        own_sum = lax.psum(own_sum, axes)

    parts = [[piece[quarter:].reshape(held, span // 4) for piece, _ in pieces] for pieces, _ in chains]
    count = len(parts[0])
    quarter_rows = jnp.concatenate(parts[0] + parts[1], axis=0)
    other = over_group(quarter_rows)
    half_rows = jnp.concatenate(
        [jnp.where(g == 0, quarter_rows, other), jnp.where(g == 0, other, quarter_rows)], axis=1
    )
    came = over_core(half_rows)
    came = jnp.concatenate([came[count * held :], came[: count * held]], axis=0)
    whole = jnp.concatenate(
        [jnp.where(c == 0, half_rows, came), jnp.where(c == 0, came, half_rows)], axis=1
    )
    spread = jnp.tile(jnp.transpose(own_sum), (1, resident))
    masked = jnp.concatenate(
        [
            jnp.where(
                slot[:, None]
                == lane_slot + jnp.where(source < 0, -(2**20), (2 * source + side) * resident),
                spread,
                0.0,
            )
            for pieces, side in chains
            for _, source in pieces
        ],
        axis=1,
    )
    masked_high, masked_low = two_terms(masked)
    whole_high, whole_low = two_terms(whole)
    update = (
        jnp.dot(masked_high, whole_high, preferred_element_type=jnp.float32)
        + jnp.dot(masked_low, whole_high, preferred_element_type=jnp.float32)
        + jnp.dot(masked_high, whole_low, preferred_element_type=jnp.float32)
    )
    return (base + (SCALING / (SHRINK_GAIN * EXPAND_GAIN)) * update).astype(jnp.bfloat16)


def solution(mesh):
    placed = (
        P(("group", "adapter"), ("tensor", "sub")),
        P(("group", "adapter")),
        P("group"),
        P(("tensor", "sub"), None),
        P(("tensor", "sub"), "adapter"),
        P("adapter", None, ("tensor", "sub")),
    )
    return jax.shard_map(
        per_device,
        mesh=mesh,
        in_specs=placed,
        out_specs=P(("group", "adapter"), ("tensor", "sub")),
        check_vma=False,
    )
```

```python
import jax
import jax.numpy as jnp
import numpy as np
from jax import lax
from jax.experimental import pallas as pl
from jax.experimental.pallas import tpu as pltpu
from jax.sharding import PartitionSpec as P

SCALING = 0.5
SHRINK_GAIN = 2.0**19
EXPAND_GAIN = 2.0**14
LANES = 128
VMEM_BYTES = 48 * 2**20


def sources(spots):
    table = []
    for half in range(spots):
        found = [half]
        if spots == 4:
            second = half - 2 if half >= 2 else half + 2
            third = half - 3 if half >= 3 else half + 3
            found += [1 if half == 0 else half - 1, second, half + 1 if half in (1, 2) else third]
        else:
            for step in range(1, spots):
                up, down = half - step, half + step
                if 2 * step > spots - 1:
                    found.append(up if half >= step else down)
                else:
                    found += [up, down]
        table.append([f if 0 <= f < spots else -(2**16) for f in found])
    return np.array(table, np.int32)


def line_steps(spots, half):
    def send(value, moves):
        return lax.ppermute(value, "adapter", [(2 * s + c, 2 * d + c) for s, d in moves for c in range(2)])

    def first(piece):
        up = send(piece, [(s, s + 1) for s in range(spots - 1)])
        down = send(piece, [(s, s - 1) for s in range(1, spots)])
        return up, down

    def rest(up, down):
        found = []
        merged = None
        if spots > 2:
            found += [up, down]
        else:
            found = [jnp.where(half >= 1, up, down)]
        for step in range(2, spots):
            goes_up = [(s, s + 1) for s in range(step - 1, spots - 1)]
            goes_down = [(s, s - 1) for s in range(1, spots - step + 1)]
            if 2 * step - 1 > spots:
                merged = send(merged, goes_up + goes_down)
            else:
                up, down = send(up, goes_up), send(down, goes_down)
                if 2 * step > spots - 1:
                    merged = jnp.where(half >= step, up, down)
                else:
                    found += [up, down]
                    continue
            found.append(merged)
        if spots == 4:
            up, down, second, third = found
            middle = (half == 1) | (half == 2)
            found = [jnp.where(half == 0, down, up), second, jnp.where(middle, down, third)]
        return found

    return first, rest


def two_terms(value):
    wide = value.astype(jnp.float32)
    high = lax.reduce_precision(wide, exponent_bits=8, mantissa_bits=7)
    return high.astype(jnp.bfloat16), (wide - high).astype(jnp.bfloat16)


def side_by_side(value):
    return jnp.concatenate(two_terms(value), axis=1)


def product_kernel(place_ref, tokens_ref, matrix_ref, out_ref):
    @pl.when(pl.program_id(0) == 0)
    def _():
        out_ref[...] = jnp.zeros_like(out_ref)

    out_ref[...] += jnp.dot(tokens_ref[...], matrix_ref[...], preferred_element_type=jnp.float32)


def base_product(tokens, matrix, place, span):
    rows, width = tokens.shape
    depth = min(width, 1024)
    return pl.pallas_call(
        product_kernel,
        grid_spec=pltpu.PrefetchScalarGridSpec(
            num_scalar_prefetch=1,
            grid=(width // depth,),
            in_specs=[
                pl.BlockSpec((rows, depth), lambda k, place: (0, k)),
                pl.BlockSpec((depth, span), lambda k, place: (k, place[0])),
            ],
            out_specs=pl.BlockSpec((rows, span), lambda k, place: (0, 0)),
        ),
        out_shape=jax.ShapeDtypeStruct((rows, span), jnp.float32),
        compiler_params=pltpu.CompilerParams(vmem_limit_bytes=VMEM_BYTES),
        cost_estimate=pl.CostEstimate(flops=0, bytes_accessed=0, transcendentals=0),
        name="base_product",
    )(jnp.reshape(place, (1,)), tokens, matrix)


PAD = 16


def pack_kernel(rows, place_ref, tokens_ref, slot_ref, *refs):
    out_ref = refs[-1]
    width = tokens_ref.shape[1]
    out_ref[:rows] = tokens_ref[...]
    tail = jnp.broadcast_to(slot_ref[...].astype(jnp.float32), (PAD, rows)).astype(out_ref.dtype)
    out_ref[rows : rows + PAD, :rows] = tail
    if width > rows:
        out_ref[rows : rows + PAD, rows:] = jnp.zeros((PAD, width - rows), out_ref.dtype)
    if len(refs) == 2:
        out_ref[rows + PAD :] = refs[0][...]


def pack_two(tokens, slot, place, quarter):
    rows = tokens.shape[0]
    return pl.pallas_call(
        lambda *refs: pack_kernel(rows, *refs),
        grid_spec=pltpu.PrefetchScalarGridSpec(
            num_scalar_prefetch=1,
            grid=(2,),
            in_specs=[
                pl.BlockSpec((rows, quarter), lambda i, place: (0, place[0] + i)),
                pl.BlockSpec((1, rows), lambda i, place: (0, 0)),
            ],
            out_specs=pl.BlockSpec((rows + PAD, quarter), lambda i, place: (0, i)),
        ),
        out_shape=jax.ShapeDtypeStruct((rows + PAD, 2 * quarter), tokens.dtype),
        cost_estimate=pl.CostEstimate(flops=0, bytes_accessed=0, transcendentals=0),
        name="pack_two",
    )(jnp.reshape(place, (1,)), tokens, slot)


def pack_core(tokens, slot, theirs, place, side, quarter):
    rows = tokens.shape[0]
    return pl.pallas_call(
        lambda *refs: pack_kernel(rows, *refs),
        grid_spec=pltpu.PrefetchScalarGridSpec(
            num_scalar_prefetch=1,
            grid=(1,),
            in_specs=[
                pl.BlockSpec((rows, quarter), lambda i, place: (0, place[0])),
                pl.BlockSpec((1, rows), lambda i, place: (0, 0)),
                pl.BlockSpec((rows + PAD, quarter), lambda i, place: (0, place[1])),
            ],
            out_specs=pl.BlockSpec((2 * (rows + PAD), quarter), lambda i, place: (0, 0)),
        ),
        out_shape=jax.ShapeDtypeStruct((2 * (rows + PAD), quarter), tokens.dtype),
        cost_estimate=pl.CostEstimate(flops=0, bytes_accessed=0, transcendentals=0),
        name="pack_core",
    )(jnp.stack([place, side]), tokens, slot, theirs)


def assemble_kernel(rows, place_ref, tokens_ref, slot_ref, theirs_ref, came_ref, every_ref, slots_ref):
    every_ref[:rows] = tokens_ref[...]
    every_ref[rows : 2 * rows] = theirs_ref[:rows]
    every_ref[2 * rows : 3 * rows] = came_ref[:rows]
    every_ref[3 * rows :] = came_ref[rows + PAD : 2 * rows + PAD]
    packed = [
        theirs_ref[rows : rows + PAD, :rows],
        came_ref[rows : rows + PAD, :rows],
        came_ref[2 * rows + PAD :, :rows],
    ]
    slots_ref[:, :rows] = slot_ref[...]
    for i, part in enumerate(packed):
        slots_ref[:, (i + 1) * rows : (i + 2) * rows] = part.astype(jnp.float32)[:1].astype(jnp.int32)


def assemble(tokens, slot, theirs, came, place, side, quarter):
    rows = tokens.shape[0]
    return pl.pallas_call(
        lambda *refs: assemble_kernel(rows, *refs),
        grid_spec=pltpu.PrefetchScalarGridSpec(
            num_scalar_prefetch=1,
            grid=(1,),
            in_specs=[
                pl.BlockSpec((rows, quarter), lambda i, place: (0, place[0])),
                pl.BlockSpec((1, rows), lambda i, place: (0, 0)),
                pl.BlockSpec((rows + PAD, quarter), lambda i, place: (0, place[1])),
                pl.BlockSpec((2 * (rows + PAD), quarter), lambda i, place: (0, 0)),
            ],
            out_specs=[
                pl.BlockSpec((4 * rows, quarter), lambda i, place: (0, 0)),
                pl.BlockSpec((1, 4 * rows), lambda i, place: (0, 0)),
            ],
        ),
        out_shape=[
            jax.ShapeDtypeStruct((4 * rows, quarter), tokens.dtype),
            jax.ShapeDtypeStruct((1, 4 * rows), jnp.int32),
        ],
        cost_estimate=pl.CostEstimate(flops=0, bytes_accessed=0, transcendentals=0),
        name="assemble",
    )(jnp.stack([place, side]), tokens, slot, theirs, came)


def shrink_kernel(rank, resident, which, first_ref, tokens_ref, slot_ref, *refs):
    weights, sums, out_ref = refs[: len(which)], refs[len(which) : -1], refs[-1]
    held = rank * resident
    count = tokens_ref.shape[0]
    tile = 256
    products = [
        jnp.dot(tokens_ref[...], w[...], preferred_element_type=jnp.float32) for w in weights
    ]
    for at in range(0, count, tile):
        slot = slot_ref[:, at : at + tile]
        total = sums[0][:, at : at + tile] if sums else jnp.zeros((rank, tile), jnp.float32)
        for product, side in zip(products, which):
            part = product[at : at + tile]
            part = jnp.transpose(part[:, :held] + part[:, held:])
            for j in range(resident):
                chosen = slot == first_ref[side] + j
                total += jnp.where(chosen, part[j * rank : (j + 1) * rank], 0.0)
        out_ref[:, at : at + tile] = total


def shrink_step(tokens, slot, weights, firsts, which, total, rank, resident):
    count, depth = tokens.shape
    sums = [] if total is None else [total]
    vmem = pl.BlockSpec(memory_space=pltpu.VMEM)
    return pl.pallas_call(
        lambda *refs: shrink_kernel(rank, resident, which, *refs),
        in_specs=[pl.BlockSpec(memory_space=pltpu.SMEM)] + [vmem] * (2 + len(weights) + len(sums)),
        out_specs=vmem,
        out_shape=jax.ShapeDtypeStruct((rank, count), jnp.float32),
        compiler_params=pltpu.CompilerParams(vmem_limit_bytes=24 * 2**20),
        cost_estimate=pl.CostEstimate(flops=0, bytes_accessed=0, transcendentals=0),
        name="shrink_step",
    )(firsts, tokens, slot, *weights, *sums)


def expand_kernel(rank, groups, scale, slots_ref, slot_ref, own_ref, came_ref, *refs):
    parts = refs[: 2 * len(groups)]
    bases, out_ref = refs[2 * len(groups) : -1], refs[-1]
    shrunk = own_ref[...] + came_ref[...]
    slot = slot_ref[...]
    update = 0.0
    at = 0
    for i, count in enumerate(groups):
        spread = jnp.concatenate(
            [jnp.where(slot == slots_ref[at + j], shrunk, 0.0) for j in range(count)], axis=0
        )
        at += count
        high = spread.astype(jnp.bfloat16)
        low = (spread - high.astype(jnp.float32)).astype(jnp.bfloat16)
        for left, right in ((high, parts[2 * i]), (low, parts[2 * i]), (high, parts[2 * i + 1])):
            update += lax.dot_general(
                left, right[...], (((0,), (0,)), ((), ())), preferred_element_type=jnp.float32
            )
    total = scale * update
    for base in bases:
        total += base[...]
    out_ref[...] = total.astype(jnp.bfloat16)


def expand_step(slots, slot, own, came, parts, bases, rank, scale):
    groups = [high.shape[0] // rank for high, _ in parts]
    flat = [term for pair in parts for term in pair]
    operands = [slot, own, came, *flat, *bases]
    rows, span = bases[0].shape
    depth = rank * sum(groups)
    return pl.pallas_call(
        lambda *refs: expand_kernel(rank, groups, scale, *refs),
        in_specs=[pl.BlockSpec(memory_space=pltpu.SMEM)]
        + [pl.BlockSpec(memory_space=pltpu.VMEM)] * len(operands),
        out_specs=pl.BlockSpec(memory_space=pltpu.VMEM),
        out_shape=jax.ShapeDtypeStruct((rows, span), jnp.bfloat16),
        compiler_params=pltpu.CompilerParams(vmem_limit_bytes=VMEM_BYTES),
        cost_estimate=pl.CostEstimate(flops=0, bytes_accessed=0, transcendentals=0),
        name="expand_step",
    )(slots, *operands)


def per_device(tokens, token_adapter_index, table, value_matrix, shrink_weight, expand_weight):
    rows, width = tokens.shape
    resident, rank, span = expand_weight.shape
    held = resident * rank
    owners = lax.axis_size("adapter")
    spots = owners // 2
    quarter = width // 4
    g, a = lax.axis_index("group"), lax.axis_index("adapter")
    c, half = a % 2, a // 2
    core_pairs = [(i, i ^ 1) for i in range(owners)]
    swap = [(0, 1), (1, 0)]
    first_step, other_steps = line_steps(spots, half)
    barrier = lax.optimization_barrier

    def over_core(value):
        return lax.ppermute(value, "adapter", core_pairs)

    def over_group(value):
        return lax.ppermute(value, "group", swap)

    def shrink_rows(side):
        return lax.dynamic_slice_in_dim(shrink_weight, (2 * g + side) * quarter, quarter, 0)

    give = (shrink_rows(1 - c) * SHRINK_GAIN).astype(jnp.float16)
    given = over_core(give)
    flat_expand = expand_weight.reshape(held, span)
    half_expand = lax.dynamic_slice_in_dim(flat_expand, g * (held // 2), held // 2, 0)
    half_expand = (half_expand * EXPAND_GAIN).astype(jnp.float16)
    blocks = [half_expand[:, i * LANES : (i + 1) * LANES] for i in range(span // LANES)]
    mine = jnp.concatenate([(shrink_rows(c) * SHRINK_GAIN).astype(jnp.float16), *blocks], axis=0)
    mine, _ = barrier((mine, give))
    mine_first = first_step(mine)

    matches = token_adapter_index[None, :] == lax.broadcasted_iota(
        jnp.int32, (table.shape[0], rows), 0
    )
    slot = jnp.sum(jnp.where(matches, table[:, None], 0), axis=0, keepdims=True)

    late_tokens, _ = barrier((tokens, mine))
    sent = pack_two(late_tokens, slot, 2 * (1 - g), quarter)
    theirs = over_group(sent)
    given_first = first_step(given)

    mine_up, mine_down, base_tokens, _ = barrier((*mine_first, tokens, sent))
    mine_first = (mine_up, mine_down)
    axes = ("tensor", "sub")
    if lax.axis_size("tensor") == 2 and lax.axis_size("sub") == 1:
        x = lax.axis_index("tensor")
        away = base_product(base_tokens, value_matrix, 1 - x, span)
        base_came = lax.ppermute(away, "tensor", swap)
        base_tokens, _ = barrier((tokens, away))
        bases = [base_product(base_tokens, value_matrix, x, span), base_came]
    else:
        partial = jnp.dot(base_tokens, value_matrix, preferred_element_type=jnp.float32)
        bases = [lax.psum_scatter(partial, axes, scatter_dimension=1, tiled=True)]

    own_mine, own_given, _ = barrier((mine, given, bases[0]))
    mine_pieces = [own_mine] + other_steps(*mine_first)
    given_pieces = [own_given] + other_steps(*given_first)
    source = jnp.asarray(sources(spots))[half]
    firsts = resident * (2 * source[:, None] + jnp.stack([c, 1 - c])[None, :]).reshape(-1)

    other_part = pack_core(tokens, slot, theirs, 2 * g + 1 - c, 1 - c, quarter)
    came = over_core(other_part)
    every, every_slot = assemble(tokens, slot, theirs, came, 2 * g + c, c, quarter)

    total = None
    for i, (mine_piece, given_piece) in enumerate(zip(mine_pieces, given_pieces)):
        weights = [side_by_side(mine_piece[:quarter]), side_by_side(given_piece)]
        if i < len(mine_pieces) - 1:
            total = shrink_step(
                every, every_slot, weights, firsts, (2 * i, 2 * i + 1), total, rank, resident
            )
        else:
            for side in range(2):
                total = shrink_step(
                    every, every_slot, weights[side : side + 1], firsts, (2 * i + side,), total, rank, resident
                )
    both_sum = total[:, : 2 * rows] + over_core(total[:, 2 * rows :])
    own_sum = both_sum[:, :rows] + over_group(both_sum[:, rows:])
    if len(bases) == 2:
        came_sum = lax.ppermute(own_sum, "tensor", swap)
    else:
        came_sum = lax.psum(own_sum, axes) - own_sum

    def expand_of(piece):
        cut = piece[quarter:].reshape(span // LANES, held // 2, LANES)
        return jnp.concatenate([cut[i] for i in range(span // LANES)], axis=1)

    here = jnp.concatenate([expand_of(piece) for piece in mine_pieces], axis=0)
    across = over_group(here)
    beside = over_core(jnp.concatenate([here, across], axis=0))
    parts = [two_terms(here), two_terms(across), two_terms(beside)]
    steps = jnp.arange(resident // 2, dtype=jnp.int32)
    sides = jnp.stack([c, 1 - c])[:, None, None, None]
    halves = jnp.stack([g, 1 - g])[None, :, None, None] * (resident // 2)
    slots = (2 * source[:, None] + sides) * resident + halves + steps
    slots = slots.astype(jnp.int32).reshape(-1)
    scale = SCALING / (SHRINK_GAIN * EXPAND_GAIN)
    return expand_step(slots, slot, own_sum, came_sum, parts, bases, rank, scale)


def solution(mesh):
    placed = (
        P(("group", "adapter"), ("tensor", "sub")),
        P(("group", "adapter")),
        P("group"),
        P(("tensor", "sub"), None),
        P(("tensor", "sub"), "adapter"),
        P("adapter", None, ("tensor", "sub")),
    )
    return jax.shard_map(
        per_device,
        mesh=mesh,
        in_specs=placed,
        out_specs=P(("group", "adapter"), ("tensor", "sub")),
        check_vma=False,
    )
```

```python
import jax
import jax.numpy as jnp
import numpy as np
from jax import lax
from jax.experimental import pallas as pl
from jax.experimental.pallas import tpu as pltpu
from jax.sharding import PartitionSpec as P

SCALING = 0.5
SHRINK_GAIN = 2.0**19
EXPAND_GAIN = 2.0**14
LANES = 128


def sources(spots):
    table = []
    for half in range(spots):
        found = [half]
        if spots == 4:
            second = half - 2 if half >= 2 else half + 2
            third = half - 3 if half >= 3 else half + 3
            found += [1 if half == 0 else half - 1, second, half + 1 if half in (1, 2) else third]
        else:
            for step in range(1, spots):
                up, down = half - step, half + step
                if 2 * step > spots - 1:
                    found.append(up if half >= step else down)
                else:
                    found += [up, down]
        table.append([f if 0 <= f < spots else -(2**16) for f in found])
    return np.array(table, np.int32)


class Line:
    def __init__(self, piece, spots, half):
        self.spots, self.half = spots, half
        self.up = self.down = piece
        self.found, self.step = [piece], 1

    def send(self, value, moves):
        return lax.ppermute(value, "adapter", [(2 * s + c, 2 * d + c) for s, d in moves for c in range(2)])

    def advance(self):
        spots, step, half = self.spots, self.step, self.half
        goes_up = [(s, s + 1) for s in range(step - 1, spots - 1)]
        goes_down = [(s, s - 1) for s in range(1, spots - step + 1)]
        self.step += 1
        if 2 * step - 1 > spots:
            self.up = self.down = self.send(self.up, goes_up + goes_down)
            self.found.append(self.up)
            return
        self.up, self.down = self.send(self.up, goes_up), self.send(self.down, goes_down)
        if 2 * step > spots - 1:
            self.up = self.down = jnp.where(half >= step, self.up, self.down)
            self.found.append(self.up)
        else:
            self.found += [self.up, self.down]

    def pieces(self):
        if self.spots != 4:
            return self.found
        own, up, down, second, third = self.found
        half = self.half
        middle = (half == 1) | (half == 2)
        return [own, jnp.where(half == 0, down, up), second, jnp.where(middle, down, third)]


def two_terms(value):
    wide = value.astype(jnp.float32)
    high = lax.reduce_precision(wide, exponent_bits=8, mantissa_bits=7)
    return high.astype(jnp.bfloat16), (wide - high).astype(jnp.bfloat16)


def side_by_side(value):
    return jnp.concatenate(two_terms(value), axis=1)


def product_kernel(span, place_ref, tokens_ref, matrix_ref, out_ref):
    columns = pl.ds(pl.multiple_of(place_ref[0] * span, LANES), span)
    out_ref[...] = jnp.dot(
        tokens_ref[...], matrix_ref[:, columns], preferred_element_type=jnp.float32
    )


def base_product(tokens, matrix, place, span):
    vmem = pl.BlockSpec(memory_space=pltpu.VMEM)
    return pl.pallas_call(
        lambda *refs: product_kernel(span, *refs),
        in_specs=[pl.BlockSpec(memory_space=pltpu.SMEM), vmem, vmem],
        out_specs=vmem,
        out_shape=jax.ShapeDtypeStruct((tokens.shape[0], span), jnp.float32),
        compiler_params=pltpu.CompilerParams(vmem_limit_bytes=16 * 2**20),
        cost_estimate=pl.CostEstimate(flops=0, bytes_accessed=0, transcendentals=0),
        name="base_product",
    )(jnp.reshape(place, (1,)), tokens, matrix)


PAD = 16


def pack_kernel(rows, place_ref, table_ref, index_ref, away_ref, *refs):
    own_ref, core_ref, slot_ref, sent_ref, kept_ref = refs
    index = index_ref[...]
    slot = jnp.zeros_like(index)
    for j in range(table_ref.shape[0]):
        slot += jnp.where(index == j, table_ref[j], 0)
    slot_ref[...] = slot
    tail = jnp.broadcast_to(slot.astype(jnp.float32), (PAD, rows)).astype(sent_ref.dtype)
    width = core_ref.shape[1]
    step = rows + PAD
    for source, out_ref, start in ((away_ref, sent_ref, 0), (own_ref, sent_ref, step), (core_ref, kept_ref, 0)):
        out_ref[start : start + rows] = source[...]
        out_ref[start + rows : start + step, :rows] = tail
        if width > rows:
            out_ref[start + rows : start + step, rows:] = jnp.zeros((PAD, width - rows), out_ref.dtype)


def pack(tokens, table, index, places, quarter):
    rows = tokens.shape[0]

    def column(i):
        return pl.BlockSpec((rows, quarter), lambda _, place: (0, place[i]))

    def whole(*shape):
        return pl.BlockSpec(shape, lambda _, place: (0, 0))

    shapes = [(1, rows), (2 * (rows + PAD), quarter), (rows + PAD, quarter)]
    return pl.pallas_call(
        lambda *refs: pack_kernel(rows, *refs),
        grid_spec=pltpu.PrefetchScalarGridSpec(
            num_scalar_prefetch=1,
            grid=(1,),
            in_specs=[pl.BlockSpec(memory_space=pltpu.SMEM), whole(1, rows), *map(column, range(3))],
            out_specs=[whole(*shape) for shape in shapes],
        ),
        out_shape=[
            jax.ShapeDtypeStruct(shapes[0], jnp.int32),
            jax.ShapeDtypeStruct(shapes[1], tokens.dtype),
            jax.ShapeDtypeStruct(shapes[2], tokens.dtype),
        ],
        cost_estimate=pl.CostEstimate(flops=0, bytes_accessed=0, transcendentals=0),
        name="pack",
    )(jnp.stack(places), table, index, tokens, tokens, tokens)


def shrink_kernel(rank, resident, rows, which, places, sums, first_ref, column_ref, *refs):
    weights = refs[-1 - sums - len(which) : len(refs) - 1 - sums]
    out_ref = refs[-1]
    held = rank * resident
    quarter = weights[0].shape[0]
    for part, (operand, row, slots) in enumerate(places):
        columns = slice(part * rows, (part + 1) * rows)
        if slots is None:
            tokens = refs[operand][row : row + rows]
            slot = refs[operand][row + rows : row + rows + PAD, :rows]
            slot = slot.astype(jnp.float32)[:1].astype(jnp.int32)
        else:
            tokens = refs[operand][:, pl.ds(pl.multiple_of(column_ref[0], quarter), quarter)]
            slot = refs[slots][...]
        total = refs[-2][:, columns] if sums else jnp.zeros((rank, rows), jnp.float32)
        for w, side in zip(weights, which):
            product = jnp.dot(tokens, w[...], preferred_element_type=jnp.float32)
            product = jnp.transpose(product[:, :held] + product[:, held:])
            for j in range(resident):
                chosen = slot == first_ref[side] + j
                total += jnp.where(chosen, product[j * rank : (j + 1) * rank], 0.0)
        out_ref[:, columns] = total


def shrink_step(operands, places, weights, firsts, column, which, sums, rows, rank, resident):
    vmem = pl.BlockSpec(memory_space=pltpu.VMEM)
    smem = pl.BlockSpec(memory_space=pltpu.SMEM)
    operands = [*operands, *weights, *sums]
    return pl.pallas_call(
        lambda *refs: shrink_kernel(rank, resident, rows, which, places, len(sums), *refs),
        in_specs=[smem, smem] + [vmem] * len(operands),
        out_specs=vmem,
        out_shape=jax.ShapeDtypeStruct((rank, len(places) * rows), jnp.float32),
        compiler_params=pltpu.CompilerParams(vmem_limit_bytes=16 * 2**20),
        cost_estimate=pl.CostEstimate(flops=0, bytes_accessed=0, transcendentals=0),
        name="shrink_step",
    )(firsts, jnp.reshape(column, (1,)), *operands)


def expand_kernel(rank, groups, scale, count, slots_ref, slot_ref, *refs):
    parts = refs[: 2 * len(groups)]
    bases, sums, out_ref = refs[2 * len(groups) : -1 - count], refs[-1 - count : -1], refs[-1]
    shrunk = sum(ref[...] for ref in sums[1:]) + sums[0][...] if count > 1 else sums[0][...]
    slot = slot_ref[...]
    update = 0.0
    at = 0
    for i, count in enumerate(groups):
        spread = jnp.concatenate(
            [jnp.where(slot == slots_ref[at + j], shrunk, 0.0) for j in range(count)], axis=0
        )
        at += count
        high = spread.astype(jnp.bfloat16)
        low = (spread - high.astype(jnp.float32)).astype(jnp.bfloat16)
        for left, right in ((high, parts[2 * i]), (low, parts[2 * i]), (high, parts[2 * i + 1])):
            update += lax.dot_general(
                left, right[...], (((0,), (0,)), ((), ())), preferred_element_type=jnp.float32
            )
    total = scale * update
    for base in bases:
        total += base[...]
    out_ref[...] = total.astype(jnp.bfloat16)


def expand_step(slots, slot, shrunk, parts, bases, rank, scale):
    groups = [high.shape[0] // rank for high, _ in parts]
    flat = [term for pair in parts for term in pair]
    operands = [slot, *flat, *bases, *shrunk]
    rows, span = bases[0].shape
    depth = rank * sum(groups)
    return pl.pallas_call(
        lambda *refs: expand_kernel(rank, groups, scale, len(shrunk), *refs),
        in_specs=[pl.BlockSpec(memory_space=pltpu.SMEM)]
        + [pl.BlockSpec(memory_space=pltpu.VMEM)] * len(operands),
        out_specs=pl.BlockSpec(memory_space=pltpu.VMEM),
        out_shape=jax.ShapeDtypeStruct((rows, span), jnp.bfloat16),
        compiler_params=pltpu.CompilerParams(vmem_limit_bytes=16 * 2**20),
        cost_estimate=pl.CostEstimate(flops=0, bytes_accessed=0, transcendentals=0),
        name="expand_step",
    )(slots, *operands)


def per_device(tokens, token_adapter_index, table, value_matrix, shrink_weight, expand_weight):
    rows, width = tokens.shape
    resident, rank, span = expand_weight.shape
    held = resident * rank
    owners = lax.axis_size("adapter")
    spots = owners // 2
    quarter = width // 4
    g, a = lax.axis_index("group"), lax.axis_index("adapter")
    c, half = a % 2, a // 2
    core_pairs = [(i, i ^ 1) for i in range(owners)]
    swap = [(0, 1), (1, 0)]
    barrier = lax.optimization_barrier

    def over_core(value):
        return lax.ppermute(value, "adapter", core_pairs)

    def over_group(value):
        return lax.ppermute(value, "group", swap)

    def shrink_rows(weight, side):
        rows_there = lax.dynamic_slice_in_dim(weight, (2 * g + side) * quarter, quarter, 0)
        return (rows_there * SHRINK_GAIN).astype(jnp.float16)

    give = shrink_rows(shrink_weight, 1 - c)
    given = over_core(give)
    shrink_later, expand_later, _ = barrier((shrink_weight, expand_weight, give))
    half_expand = lax.dynamic_slice_in_dim(
        expand_later.reshape(held, span), g * (held // 2), held // 2, 0
    )
    half_expand = (half_expand * EXPAND_GAIN).astype(jnp.float16)
    blocks = [half_expand[:, i * LANES : (i + 1) * LANES] for i in range(span // LANES)]
    mine = jnp.concatenate([shrink_rows(shrink_later, c), *blocks], axis=0)
    mine_line = Line(mine, spots, half)
    mine_line.advance()

    later, _ = barrier((tokens, mine))
    places = [2 * (1 - g) + 1 - c, 2 * (1 - g) + c, 2 * g + 1 - c]
    slot, sent, kept = pack(later, table, token_adapter_index[None, :], places, quarter)
    theirs = over_group(sent)
    given_line = Line(given, spots, half)
    given_line.advance()
    came_own = over_core(kept)
    came_theirs = over_core(theirs[: rows + PAD])

    source = jnp.asarray(sources(spots))[half]
    firsts = resident * (2 * source[:, None] + jnp.stack([c, 1 - c])[None, :]).reshape(-1)
    if spots > 2:
        mine_line.advance()
        given_line.advance()

    base_tokens, came_own, mine_line.up, mine_line.down = barrier(
        (tokens, came_own, mine_line.up, mine_line.down)
    )
    axes = ("tensor", "sub")
    if lax.axis_size("tensor") == 2 and lax.axis_size("sub") == 1:
        x = lax.axis_index("tensor")
        away = base_product(base_tokens, value_matrix, 1 - x, span)
        base_came = lax.ppermute(away, "tensor", swap)
        base_tokens, _ = barrier((tokens, away))
        bases = [base_product(base_tokens, value_matrix, x, span), base_came]
    else:
        partial = jnp.dot(base_tokens, value_matrix, preferred_element_type=jnp.float32)
        bases = [lax.psum_scatter(partial, axes, scatter_dimension=1, tiled=True)]

    for _ in range(spots - 3):
        mine_line.advance()
        given_line.advance()
    mine_pieces, given_pieces = mine_line.pieces(), given_line.pieces()

    column = (2 * g + c) * quarter

    def weights_of(start, stop):
        weights = []
        for i in range(start, stop):
            weights += [side_by_side(mine_pieces[i][:quarter]), side_by_side(given_pieces[i])]
        return weights

    def products(operands, places, weights, start, sums):
        which = list(range(2 * start, 2 * start + len(weights)))
        return shrink_step(
            operands, places, weights, firsts, column, which, sums, rows, rank, resident
        )

    here_parts = ((tokens, slot, came_own), ((0, 0, 1), (2, 0, None)))
    there_parts = ((theirs, came_theirs), ((0, rows + PAD, None), (1, 0, None)))
    all_parts = (
        (tokens, slot, came_own, theirs, came_theirs),
        ((0, 0, 1), (3, rows + PAD, None), (2, 0, None), (4, 0, None)),
    )

    last = len(mine_pieces) - 1
    here_sum = there_sum = None
    for start in range(0, last, 3):
        weights = weights_of(start, min(start + 3, last))
        here_sum = products(*here_parts, weights, start, [] if start == 0 else [here_sum])
        there_sum = products(*there_parts, weights, start, [] if start == 0 else [there_sum])
    expand_pieces = mine_pieces
    if spots == 4:
        mine_line.found[-1], given_line.found[-1], here_sum, there_sum = barrier(
            (mine_line.found[-1], given_line.found[-1], here_sum, there_sum)
        )
        mine_pieces, given_pieces = mine_line.pieces(), given_line.pieces()
    before = jnp.concatenate(
        [here_sum[:, :rows], there_sum[:, :rows], here_sum[:, rows:], there_sum[:, rows:]], axis=1
    )
    total = products(*all_parts, weights_of(last, last + 1), last, [before])
    both_sum = total[:, : 2 * rows] + over_core(total[:, 2 * rows :])
    own_sum, other_sum = both_sum[:, :rows], both_sum[:, rows:]
    if len(bases) == 2:
        across = [(i, 3 - i) for i in range(4)]
        shrunk = [
            own_sum,
            lax.ppermute(other_sum, ("group", "tensor"), across),
            over_group(other_sum),
            lax.ppermute(own_sum, "tensor", swap),
        ]
    else:
        shrunk = [lax.psum(own_sum + over_group(other_sum), axes)]

    def expand_of(piece):
        cut = piece[quarter:].reshape(span // LANES, held // 2, LANES)
        return jnp.concatenate([cut[i] for i in range(span // LANES)], axis=1)

    here = jnp.concatenate([expand_of(piece) for piece in expand_pieces], axis=0)
    across = over_group(here)
    beside = over_core(jnp.concatenate([here, across], axis=0))
    terms = [two_terms(here), two_terms(across), two_terms(beside)]
    steps = jnp.arange(resident // 2, dtype=jnp.int32)
    sides = jnp.stack([c, 1 - c])[:, None, None, None]
    halves = jnp.stack([g, 1 - g])[None, :, None, None] * (resident // 2)
    slots = (2 * source[:, None] + sides) * resident + halves + steps
    slots = slots.astype(jnp.int32).reshape(-1)
    scale = SCALING / (SHRINK_GAIN * EXPAND_GAIN)
    return expand_step(slots, slot, shrunk, terms, bases, rank, scale)


def solution(mesh):
    placed = (
        P(("group", "adapter"), ("tensor", "sub")),
        P(("group", "adapter")),
        P("group"),
        P(("tensor", "sub"), None),
        P(("tensor", "sub"), "adapter"),
        P("adapter", None, ("tensor", "sub")),
    )
    return jax.shard_map(
        per_device,
        mesh=mesh,
        in_specs=placed,
        out_specs=P(("group", "adapter"), ("tensor", "sub")),
        check_vma=False,
    )
```

```python
import jax
import jax.numpy as jnp
import numpy as np
from jax import lax
from jax.experimental import pallas as pl
from jax.experimental.pallas import tpu as pltpu
from jax.sharding import PartitionSpec as P

SCALING = 0.5
SHRINK_GAIN = 2.0**19
EXPAND_GAIN = 2.0**14
LANES = 128


def sources(spots):
    if spots == 4:
        return np.array([[0, 1, 2, 3], [1, 0, 2, 3], [2, 3, 1, 0], [3, 2, 1, 0]], np.int32)
    table = []
    for half in range(spots):
        found = [half]
        for step in range(1, spots):
            up, down = half - step, half + step
            if 2 * step > spots - 1:
                found.append(up if half >= step else down)
            else:
                found += [up, down]
        table.append([f if 0 <= f < spots else -(2**16) for f in found])
    return np.array(table, np.int32)


class FourLine:
    def __init__(self, piece, half):
        self.own, self.half = piece, half

    def send(self, value, moves):
        return lax.ppermute(value, "adapter", [(2 * s + c, 2 * d + c) for s, d in moves for c in range(2)])

    def first(self):
        self.end = self.send(self.own, [(0, 1), (1, 0), (2, 3), (3, 2)])
        self.middle = self.send(self.own, [(1, 2), (2, 1)])

    def second(self):
        self.far_middle = self.send(self.end, [(1, 2), (2, 1)])
        self.far_end = self.send(self.middle, [(1, 0), (2, 3)])

    def third(self):
        self.last = self.send(self.far_middle, [(1, 0), (2, 3)])

    def pieces(self):
        inner = (self.half == 1) | (self.half == 2)
        return [
            self.own,
            self.end,
            jnp.where(inner, self.middle, self.far_end),
            jnp.where(inner, self.far_middle, self.last),
        ]


class Line:
    def __init__(self, piece, spots, half):
        self.spots, self.half = spots, half
        self.up = self.down = piece
        self.found, self.step = [piece], 1

    def send(self, value, moves):
        return lax.ppermute(value, "adapter", [(2 * s + c, 2 * d + c) for s, d in moves for c in range(2)])

    def advance(self):
        spots, step, half = self.spots, self.step, self.half
        goes_up = [(s, s + 1) for s in range(step - 1, spots - 1)]
        goes_down = [(s, s - 1) for s in range(1, spots - step + 1)]
        self.step += 1
        if 2 * step - 1 > spots:
            self.up = self.down = self.send(self.up, goes_up + goes_down)
            self.found.append(self.up)
            return
        self.up, self.down = self.send(self.up, goes_up), self.send(self.down, goes_down)
        if 2 * step > spots - 1:
            self.up = self.down = jnp.where(half >= step, self.up, self.down)
            self.found.append(self.up)
        else:
            self.found += [self.up, self.down]

    def pieces(self):
        return self.found


def two_terms(value):
    wide = value.astype(jnp.float32)
    high = lax.reduce_precision(wide, exponent_bits=8, mantissa_bits=7)
    return high.astype(jnp.bfloat16), (wide - high).astype(jnp.bfloat16)


def side_by_side(value):
    return jnp.concatenate(two_terms(value), axis=1)


def product_kernel(span, pieces, place_ref, tokens_ref, matrix_ref, *refs):
    out_refs, (tokens_here, matrix_here, token_sems, matrix_sems) = refs[:2], refs[2:]
    depth = tokens_ref.shape[1] // pieces
    parts = [pl.ds(k * depth, depth) for k in range(pieces)]
    copies = [[], []]
    for i in range(2):
        columns = pl.ds(pl.multiple_of(place_ref[i] * span, LANES), span)
        for k, part in enumerate(parts):
            arriving = []
            if i == 0:
                arriving.append(
                    pltpu.make_async_copy(
                        tokens_ref.at[:, part], tokens_here.at[:, part], token_sems.at[k]
                    )
                )
            arriving.append(
                pltpu.make_async_copy(
                    matrix_ref.at[part, columns], matrix_here.at[i, part], matrix_sems.at[i, k]
                )
            )
            for copy in arriving:
                copy.start()
            copies[i].append(arriving)
    for i, out_ref in enumerate(out_refs):
        total = 0.0
        for k, part in enumerate(parts):
            for copy in copies[i][k]:
                copy.wait()
            total += jnp.dot(
                tokens_here[:, part], matrix_here[i, part], preferred_element_type=jnp.float32
            )
        out_ref[...] = total


def base_product(tokens, matrix, places, span):
    rows, width = tokens.shape
    pieces = 4
    vmem, hbm = pl.BlockSpec(memory_space=pltpu.VMEM), pl.BlockSpec(memory_space=pltpu.HBM)
    return pl.pallas_call(
        lambda *refs: product_kernel(span, pieces, *refs),
        in_specs=[pl.BlockSpec(memory_space=pltpu.SMEM), hbm, hbm],
        out_specs=[vmem] * 2,
        out_shape=[jax.ShapeDtypeStruct((rows, span), jnp.float32)] * 2,
        scratch_shapes=[
            pltpu.VMEM((rows, width), tokens.dtype),
            pltpu.VMEM((2, width, span), matrix.dtype),
            pltpu.SemaphoreType.DMA((pieces,)),
            pltpu.SemaphoreType.DMA((2, pieces)),
        ],
        compiler_params=pltpu.CompilerParams(vmem_limit_bytes=52 * 2**20),
        cost_estimate=pl.CostEstimate(flops=0, bytes_accessed=0, transcendentals=0),
        name="base_product",
    )(jnp.stack(places), tokens, matrix)


PAD = 16


def pack_kernel(rows, place_ref, table_ref, index_ref, away_ref, *refs):
    own_ref, core_ref, slot_ref, sent_ref, kept_ref = refs
    index = index_ref[...]
    slot = jnp.zeros_like(index)
    for j in range(table_ref.shape[0]):
        slot += jnp.where(index == j, table_ref[j], 0)
    slot_ref[...] = slot
    tail = jnp.broadcast_to(slot.astype(jnp.float32), (PAD, rows)).astype(sent_ref.dtype)
    width = core_ref.shape[1]
    step = rows + PAD
    for source, out_ref, start in ((away_ref, sent_ref, 0), (own_ref, sent_ref, step), (core_ref, kept_ref, 0)):
        out_ref[start : start + rows] = source[...]
        out_ref[start + rows : start + step, :rows] = tail
        if width > rows:
            out_ref[start + rows : start + step, rows:] = jnp.zeros((PAD, width - rows), out_ref.dtype)


def pack(tokens, table, index, places, quarter):
    rows = tokens.shape[0]

    def column(i):
        return pl.BlockSpec((rows, quarter), lambda _, place: (0, place[i]))

    def whole(*shape):
        return pl.BlockSpec(shape, lambda _, place: (0, 0))

    shapes = [(1, rows), (2 * (rows + PAD), quarter), (rows + PAD, quarter)]
    return pl.pallas_call(
        lambda *refs: pack_kernel(rows, *refs),
        grid_spec=pltpu.PrefetchScalarGridSpec(
            num_scalar_prefetch=1,
            grid=(1,),
            in_specs=[pl.BlockSpec(memory_space=pltpu.SMEM), whole(1, rows), *map(column, range(3))],
            out_specs=[whole(*shape) for shape in shapes],
        ),
        out_shape=[
            jax.ShapeDtypeStruct(shapes[0], jnp.int32),
            jax.ShapeDtypeStruct(shapes[1], tokens.dtype),
            jax.ShapeDtypeStruct(shapes[2], tokens.dtype),
        ],
        cost_estimate=pl.CostEstimate(flops=0, bytes_accessed=0, transcendentals=0),
        name="pack",
    )(jnp.stack(places), table, index, tokens, tokens, tokens)


def shrink_kernel(rank, resident, rows, which, places, sums, first_ref, column_ref, *refs):
    weights = refs[-1 - sums - len(which) : len(refs) - 1 - sums]
    out_ref = refs[-1]
    held = rank * resident
    quarter = weights[0].shape[0]
    for part, (operand, row, slots) in enumerate(places):
        columns = slice(part * rows, (part + 1) * rows)
        if slots is None:
            tokens = refs[operand][row : row + rows]
            slot = refs[operand][row + rows : row + rows + PAD, :rows]
            slot = slot.astype(jnp.float32)[:1].astype(jnp.int32)
        else:
            tokens = refs[operand][:, pl.ds(pl.multiple_of(column_ref[0], quarter), quarter)]
            slot = refs[slots][...]
        total = refs[-2][:, columns] if sums else jnp.zeros((rank, rows), jnp.float32)
        for w, side in zip(weights, which):
            product = jnp.dot(tokens, w[...], preferred_element_type=jnp.float32)
            product = jnp.transpose(product[:, :held] + product[:, held:])
            for j in range(resident):
                chosen = slot == first_ref[side] + j
                total += jnp.where(chosen, product[j * rank : (j + 1) * rank], 0.0)
        out_ref[:, columns] = total


def shrink_step(operands, places, weights, firsts, column, which, sums, rows, rank, resident):
    vmem = pl.BlockSpec(memory_space=pltpu.VMEM)
    smem = pl.BlockSpec(memory_space=pltpu.SMEM)
    operands = [*operands, *weights, *sums]
    return pl.pallas_call(
        lambda *refs: shrink_kernel(rank, resident, rows, which, places, len(sums), *refs),
        in_specs=[smem, smem] + [vmem] * len(operands),
        out_specs=vmem,
        out_shape=jax.ShapeDtypeStruct((rank, len(places) * rows), jnp.float32),
        compiler_params=pltpu.CompilerParams(vmem_limit_bytes=16 * 2**20),
        cost_estimate=pl.CostEstimate(flops=0, bytes_accessed=0, transcendentals=0),
        name="shrink_step",
    )(firsts, jnp.reshape(column, (1,)), *operands)


def expand_kernel(rank, groups, scale, count, slots_ref, slot_ref, *refs):
    parts = refs[: 2 * len(groups)]
    bases, sums, out_ref = refs[2 * len(groups) : -1 - count], refs[-1 - count : -1], refs[-1]
    shrunk = sum(ref[...] for ref in sums[1:]) + sums[0][...] if count > 1 else sums[0][...]
    slot = slot_ref[...]
    update = 0.0
    at = 0
    for i, count in enumerate(groups):
        spread = jnp.concatenate(
            [jnp.where(slot == slots_ref[at + j], shrunk, 0.0) for j in range(count)], axis=0
        )
        at += count
        high = spread.astype(jnp.bfloat16)
        low = (spread - high.astype(jnp.float32)).astype(jnp.bfloat16)
        for left, right in ((high, parts[2 * i]), (low, parts[2 * i]), (high, parts[2 * i + 1])):
            update += lax.dot_general(
                left, right[...], (((0,), (0,)), ((), ())), preferred_element_type=jnp.float32
            )
    total = scale * update
    for base in bases:
        total += base[...]
    out_ref[...] = total.astype(jnp.bfloat16)


def expand_step(slots, slot, shrunk, parts, bases, rank, scale):
    groups = [high.shape[0] // rank for high, _ in parts]
    flat = [term for pair in parts for term in pair]
    operands = [slot, *flat, *bases, *shrunk]
    rows, span = bases[0].shape
    depth = rank * sum(groups)
    return pl.pallas_call(
        lambda *refs: expand_kernel(rank, groups, scale, len(shrunk), *refs),
        in_specs=[pl.BlockSpec(memory_space=pltpu.SMEM)]
        + [pl.BlockSpec(memory_space=pltpu.VMEM)] * len(operands),
        out_specs=pl.BlockSpec(memory_space=pltpu.VMEM),
        out_shape=jax.ShapeDtypeStruct((rows, span), jnp.bfloat16),
        compiler_params=pltpu.CompilerParams(vmem_limit_bytes=16 * 2**20),
        cost_estimate=pl.CostEstimate(flops=0, bytes_accessed=0, transcendentals=0),
        name="expand_step",
    )(slots, *operands)


def per_device(tokens, token_adapter_index, table, value_matrix, shrink_weight, expand_weight):
    rows, width = tokens.shape
    resident, rank, span = expand_weight.shape
    held = resident * rank
    owners = lax.axis_size("adapter")
    spots = owners // 2
    quarter = width // 4
    g, a = lax.axis_index("group"), lax.axis_index("adapter")
    c, half = a % 2, a // 2
    core_pairs = [(i, i ^ 1) for i in range(owners)]
    swap = [(0, 1), (1, 0)]
    barrier = lax.optimization_barrier

    def over_core(value):
        return lax.ppermute(value, "adapter", core_pairs)

    def over_group(value):
        return lax.ppermute(value, "group", swap)

    def shrink_rows(weight, side):
        rows_there = lax.dynamic_slice_in_dim(weight, (2 * g + side) * quarter, quarter, 0)
        return (rows_there * SHRINK_GAIN).astype(jnp.float16)

    give = shrink_rows(shrink_weight, 1 - c)
    given = over_core(give)
    shrink_later, expand_later, _ = barrier((shrink_weight, expand_weight, give))
    half_expand = lax.dynamic_slice_in_dim(
        expand_later.reshape(held, span), g * (held // 2), held // 2, 0
    )
    half_expand = (half_expand * EXPAND_GAIN).astype(jnp.float16)
    blocks = [half_expand[:, i * LANES : (i + 1) * LANES] for i in range(span // LANES)]
    mine = jnp.concatenate([shrink_rows(shrink_later, c), *blocks], axis=0)
    four = spots == 4
    if four:
        mine_line = FourLine(mine, half)
        mine_line.first()
    else:
        mine_line = Line(mine, spots, half)
        mine_line.advance()

    later, _ = barrier((tokens, mine))
    places = [2 * (1 - g) + 1 - c, 2 * (1 - g) + c, 2 * g + 1 - c]
    slot, sent, kept = pack(later, table, token_adapter_index[None, :], places, quarter)
    theirs = over_group(sent)
    if four:
        given_line = FourLine(given, half)
        given_line.first()
    else:
        given_line = Line(given, spots, half)
        given_line.advance()
    came_theirs = over_core(theirs[: rows + PAD])

    source = jnp.asarray(sources(spots))[half]
    firsts = resident * (2 * source[:, None] + jnp.stack([c, 1 - c])[None, :]).reshape(-1)
    base_tokens = tokens
    if four:
        mine_line.second()
        given_line.second()
        given_line.far_middle, base_tokens, kept = barrier((given_line.far_middle, tokens, kept))
    came_own = over_core(kept)

    axes = ("tensor", "sub")
    if lax.axis_size("tensor") == 2 and lax.axis_size("sub") == 1:
        x = lax.axis_index("tensor")
        away, own_base = base_product(base_tokens, value_matrix, [1 - x, x], span)
        bases = [own_base, lax.ppermute(away, "tensor", swap)]
    else:
        partial = jnp.dot(base_tokens, value_matrix, preferred_element_type=jnp.float32)
        bases = [lax.psum_scatter(partial, axes, scatter_dimension=1, tiled=True)]

    if four:
        mine_line.third()
        given_line.third()
    else:
        for _ in range(spots - 2):
            mine_line.advance()
            given_line.advance()
    mine_pieces, given_pieces = mine_line.pieces(), given_line.pieces()

    column = (2 * g + c) * quarter

    def weights_of(start, stop):
        weights = []
        for i in range(start, stop):
            weights += [side_by_side(mine_pieces[i][:quarter]), side_by_side(given_pieces[i])]
        return weights

    def products(operands, places, weights, start, sums):
        which = list(range(start, start + len(weights)))
        return shrink_step(
            operands, places, weights, firsts, column, which, sums, rows, rank, resident
        )

    here_parts = ((tokens, slot, came_own), ((0, 0, 1), (2, 0, None)))
    there_parts = ((theirs, came_theirs), ((0, rows + PAD, None), (1, 0, None)))
    all_parts = (
        (tokens, slot, came_own, theirs, came_theirs),
        ((0, 0, 1), (3, rows + PAD, None), (2, 0, None), (4, 0, None)),
    )

    last = len(mine_pieces) - 1
    here_sum = there_sum = None
    for start in range(0, last, 3):
        weights = weights_of(start, min(start + 3, last))
        here_sum = products(*here_parts, weights, 2 * start, [] if start == 0 else [here_sum])
        there_sum = products(*there_parts, weights, 2 * start, [] if start == 0 else [there_sum])
    late_mine, late_given = mine_pieces, given_pieces
    if four:
        mine_line.last, given_line.last, here_sum, there_sum = barrier(
            (mine_line.last, given_line.last, here_sum, there_sum)
        )
        late_mine, late_given = mine_line.pieces(), given_line.pieces()
    total = jnp.concatenate(
        [here_sum[:, :rows], there_sum[:, :rows], here_sum[:, rows:], there_sum[:, rows:]], axis=1
    )
    total = products(*all_parts, [side_by_side(late_mine[last][:quarter])], 2 * last, [total])
    if four:
        given_line.last, total = barrier((given_line.last, total))
        late_given = given_line.pieces()
    almost = total
    total = products(*all_parts, [side_by_side(late_given[last])], 2 * last + 1, [total])
    both_sum = total[:, : 2 * rows] + over_core(total[:, 2 * rows :])
    own_sum, other_sum = both_sum[:, :rows], both_sum[:, rows:]
    if len(bases) == 2:
        across = [(i, 3 - i) for i in range(4)]
        shrunk = [
            own_sum,
            lax.ppermute(other_sum, ("group", "tensor"), across),
            over_group(other_sum),
            lax.ppermute(own_sum, "tensor", swap),
        ]
    else:
        shrunk = [lax.psum(own_sum + over_group(other_sum), axes)]

    def expand_of(piece):
        cut = piece[quarter:].reshape(span // LANES, held // 2, LANES)
        return jnp.concatenate([cut[i] for i in range(span // LANES)], axis=1)

    here = jnp.concatenate([expand_of(piece) for piece in mine_pieces], axis=0)
    across, _ = barrier((over_group(here), almost))
    beside = over_core(jnp.concatenate([here, across], axis=0))
    terms = [two_terms(here), two_terms(across), two_terms(beside)]
    steps = jnp.arange(resident // 2, dtype=jnp.int32)
    sides = jnp.stack([c, 1 - c])[:, None, None, None]
    halves = jnp.stack([g, 1 - g])[None, :, None, None] * (resident // 2)
    slots = (2 * source[:, None] + sides) * resident + halves + steps
    slots = slots.astype(jnp.int32).reshape(-1)
    scale = SCALING / (SHRINK_GAIN * EXPAND_GAIN)
    return expand_step(slots, slot, shrunk, terms, bases, rank, scale)


def solution(mesh):
    placed = (
        P(("group", "adapter"), ("tensor", "sub")),
        P(("group", "adapter")),
        P("group"),
        P(("tensor", "sub"), None),
        P(("tensor", "sub"), "adapter"),
        P("adapter", None, ("tensor", "sub")),
    )
    return jax.shard_map(
        per_device,
        mesh=mesh,
        in_specs=placed,
        out_specs=P(("group", "adapter"), ("tensor", "sub")),
        check_vma=False,
    )
```

```python
import jax
import jax.numpy as jnp
import numpy as np
from jax import lax
from jax.experimental import pallas as pl
from jax.experimental.pallas import tpu as pltpu
from jax.sharding import PartitionSpec as P

SCALING = 0.5
SHRINK_GAIN = 2.0**19
EXPAND_GAIN = 2.0**14
LANES = 128


def sources(spots):
    if spots == 4:
        return np.array([[0, 1, 2, 3], [1, 0, 2, 3], [2, 3, 1, 0], [3, 2, 1, 0]], np.int32)
    table = []
    for half in range(spots):
        found = [half]
        for step in range(1, spots):
            up, down = half - step, half + step
            if 2 * step > spots - 1:
                found.append(up if half >= step else down)
            else:
                found += [up, down]
        table.append([f if 0 <= f < spots else -(2**16) for f in found])
    return np.array(table, np.int32)


class FourLine:
    def __init__(self, piece, half):
        self.own, self.half = piece, half

    def send(self, value, moves):
        return lax.ppermute(value, "adapter", [(2 * s + c, 2 * d + c) for s, d in moves for c in range(2)])

    def first(self):
        self.end = self.send(self.own, [(0, 1), (1, 0), (2, 3), (3, 2)])
        self.middle = self.send(self.own, [(1, 2), (2, 1)])

    def second(self):
        self.far_middle = self.send(self.end, [(1, 2), (2, 1)])
        self.far_end = self.send(self.middle, [(1, 0), (2, 3)])

    def third(self):
        self.last = self.send(self.far_middle, [(1, 0), (2, 3)])

    def pieces(self):
        inner = (self.half == 1) | (self.half == 2)
        return [
            self.own,
            self.end,
            jnp.where(inner, self.middle, self.far_end),
            jnp.where(inner, self.far_middle, self.last),
        ]


class Line:
    def __init__(self, piece, spots, half):
        self.spots, self.half = spots, half
        self.up = self.down = piece
        self.found, self.step = [piece], 1

    def send(self, value, moves):
        return lax.ppermute(value, "adapter", [(2 * s + c, 2 * d + c) for s, d in moves for c in range(2)])

    def advance(self):
        spots, step, half = self.spots, self.step, self.half
        goes_up = [(s, s + 1) for s in range(step - 1, spots - 1)]
        goes_down = [(s, s - 1) for s in range(1, spots - step + 1)]
        self.step += 1
        if 2 * step - 1 > spots:
            self.up = self.down = self.send(self.up, goes_up + goes_down)
            self.found.append(self.up)
            return
        self.up, self.down = self.send(self.up, goes_up), self.send(self.down, goes_down)
        if 2 * step > spots - 1:
            self.up = self.down = jnp.where(half >= step, self.up, self.down)
            self.found.append(self.up)
        else:
            self.found += [self.up, self.down]

    def pieces(self):
        return self.found


def two_terms(value):
    wide = value.astype(jnp.float32)
    high = lax.reduce_precision(wide, exponent_bits=8, mantissa_bits=7)
    return high.astype(jnp.bfloat16), (wide - high).astype(jnp.bfloat16)


def side_by_side(value):
    return jnp.concatenate(two_terms(value), axis=1)


def product_kernel(span, pieces, place_ref, tokens_ref, matrix_ref, *refs):
    out_refs, (tokens_here, matrix_here, token_sems, matrix_sems) = refs[:-4], refs[-4:]
    depth = tokens_ref.shape[1] // pieces
    parts = [pl.ds(k * depth, depth) for k in range(pieces)]
    copies = [[] for _ in out_refs]
    for i in range(len(out_refs)):
        columns = pl.ds(pl.multiple_of(place_ref[i] * span, LANES), span)
        for k, part in enumerate(parts):
            arriving = []
            if i == 0:
                arriving.append(
                    pltpu.make_async_copy(
                        tokens_ref.at[:, part], tokens_here.at[:, part], token_sems.at[k]
                    )
                )
            arriving.append(
                pltpu.make_async_copy(
                    matrix_ref.at[part, columns], matrix_here.at[i, part], matrix_sems.at[i, k]
                )
            )
            for copy in arriving:
                copy.start()
            copies[i].append(arriving)
    for i, out_ref in enumerate(out_refs):
        total = 0.0
        for k, part in enumerate(parts):
            for copy in copies[i][k]:
                copy.wait()
            total += jnp.dot(
                tokens_here[:, part], matrix_here[i, part], preferred_element_type=jnp.float32
            )
        out_ref[...] = total


def base_product(tokens, matrix, places, span):
    rows, width = tokens.shape
    pieces = 4
    vmem, hbm = pl.BlockSpec(memory_space=pltpu.VMEM), pl.BlockSpec(memory_space=pltpu.HBM)
    return pl.pallas_call(
        lambda *refs: product_kernel(span, pieces, *refs),
        in_specs=[pl.BlockSpec(memory_space=pltpu.SMEM), hbm, hbm],
        out_specs=[vmem] * len(places),
        out_shape=[jax.ShapeDtypeStruct((rows, span), jnp.float32)] * len(places),
        scratch_shapes=[
            pltpu.VMEM((rows, width), tokens.dtype),
            pltpu.VMEM((len(places), width, span), matrix.dtype),
            pltpu.SemaphoreType.DMA((pieces,)),
            pltpu.SemaphoreType.DMA((len(places), pieces)),
        ],
        compiler_params=pltpu.CompilerParams(vmem_limit_bytes=52 * 2**20),
        cost_estimate=pl.CostEstimate(flops=0, bytes_accessed=0, transcendentals=0),
        name="base_product",
    )(jnp.stack(places), tokens, matrix)


PAD = 16


def pack_kernel(rows, place_ref, table_ref, index_ref, away_ref, *refs):
    own_ref, core_ref, slot_ref, sent_ref, kept_ref = refs
    index = index_ref[...]
    slot = jnp.zeros_like(index)
    for j in range(table_ref.shape[0]):
        slot += jnp.where(index == j, table_ref[j], 0)
    slot_ref[...] = slot
    tail = jnp.broadcast_to(slot.astype(jnp.float32), (PAD, rows)).astype(sent_ref.dtype)
    width = core_ref.shape[1]
    step = rows + PAD
    for source, out_ref, start in ((away_ref, sent_ref, 0), (own_ref, sent_ref, step), (core_ref, kept_ref, 0)):
        out_ref[start : start + rows] = source[...]
        out_ref[start + rows : start + step, :rows] = tail
        if width > rows:
            out_ref[start + rows : start + step, rows:] = jnp.zeros((PAD, width - rows), out_ref.dtype)


def pack(tokens, table, index, places, quarter):
    rows = tokens.shape[0]

    def column(i):
        return pl.BlockSpec((rows, quarter), lambda _, place: (0, place[i]))

    def whole(*shape):
        return pl.BlockSpec(shape, lambda _, place: (0, 0))

    shapes = [(1, rows), (2 * (rows + PAD), quarter), (rows + PAD, quarter)]
    return pl.pallas_call(
        lambda *refs: pack_kernel(rows, *refs),
        grid_spec=pltpu.PrefetchScalarGridSpec(
            num_scalar_prefetch=1,
            grid=(1,),
            in_specs=[pl.BlockSpec(memory_space=pltpu.SMEM), whole(1, rows), *map(column, range(3))],
            out_specs=[whole(*shape) for shape in shapes],
        ),
        out_shape=[
            jax.ShapeDtypeStruct(shapes[0], jnp.int32),
            jax.ShapeDtypeStruct(shapes[1], tokens.dtype),
            jax.ShapeDtypeStruct(shapes[2], tokens.dtype),
        ],
        cost_estimate=pl.CostEstimate(flops=0, bytes_accessed=0, transcendentals=0),
        name="pack",
    )(jnp.stack(places), table, index, tokens, tokens, tokens)


def shrink_kernel(rank, resident, rows, which, places, mode, first_ref, column_ref, *refs):
    held = rank * resident
    count = 1 + max(max(p[0], p[2] or 0) for p in places)
    operands, refs = refs[:count], refs[count:]
    weights, refs = refs[: len(which)], refs[len(which) :]
    quarter = weights[0].shape[0]
    group = lax.broadcasted_iota(jnp.int32, (1, held), 1) // rank

    def rows_of(arrays, part):
        per = arrays[0].shape[0] // rows
        return arrays[part // per][part % per * rows : (part % per + 1) * rows]

    if mode:
        outs = refs[-mode:]
        inputs = refs[:-mode]
        slot_rows = inputs[-(len(places) // 2) :]
        sums = inputs[: -(len(places) // 2)]
    for part, (operand, row, slots) in enumerate(places):
        if slots is None:
            tokens = operands[operand][row : row + rows]
        else:
            tokens = operands[operand][:, pl.ds(pl.multiple_of(column_ref[0], quarter), quarter)]
        if mode:
            slot = rows_of(slot_rows, part)
            total = rows_of(sums, part)
        else:
            if slots is None:
                slot = operands[operand][row + rows : row + rows + PAD, :rows].astype(jnp.float32)[:1]
            else:
                slot = operands[slots][...].astype(jnp.float32)
            slot = jnp.transpose(jnp.broadcast_to(slot, (held, rows))).astype(jnp.int32)
            refs[1][part * rows : (part + 1) * rows] = slot
            total = jnp.zeros((rows, held), jnp.float32)
        for w, side in zip(weights, which):
            product = jnp.dot(tokens, w[...], preferred_element_type=jnp.float32)
            chosen = slot == first_ref[side] + group
            total = jnp.where(chosen, product[:, :held] + product[:, held:], total)
        if mode < 2:
            out_ref = outs[0] if mode else refs[0]
            out_ref[part * rows : (part + 1) * rows] = total
        else:
            total = jnp.transpose(total)
            gathered = total[:rank]
            for j in range(1, resident):
                gathered += total[j * rank : (j + 1) * rank]
            at = part // 2 * rows
            outs[part % 2][:, at : at + rows] = gathered


def shrink_step(operands, places, weights, firsts, column, which, sums, slots, mode, rows, rank, resident):
    vmem = pl.BlockSpec(memory_space=pltpu.VMEM)
    smem = pl.BlockSpec(memory_space=pltpu.SMEM)
    operands = [*operands, *weights, *sums, *slots]
    count, held = len(places) * rows, rank * resident
    wide = jax.ShapeDtypeStruct((count, held), jnp.float32)
    narrow = jax.ShapeDtypeStruct((rank, count // 2), jnp.float32)
    shapes = [[wide, jax.ShapeDtypeStruct((count, held), jnp.int32)], [wide], [narrow, narrow]][mode]
    return pl.pallas_call(
        lambda *refs: shrink_kernel(rank, resident, rows, which, places, mode, *refs),
        in_specs=[smem, smem] + [vmem] * len(operands),
        out_specs=[vmem] * len(shapes),
        out_shape=shapes,
        compiler_params=pltpu.CompilerParams(vmem_limit_bytes=16 * 2**20),
        cost_estimate=pl.CostEstimate(flops=0, bytes_accessed=0, transcendentals=0),
        name="shrink_step",
    )(firsts, jnp.reshape(column, (1,)), *operands)


def expand_kernel(rank, groups, scale, count, slots_ref, slot_ref, *refs):
    parts = refs[: 2 * len(groups)]
    bases, sums, out_ref = refs[2 * len(groups) : -1 - count], refs[-1 - count : -1], refs[-1]
    shrunk = sums[0][...]
    for ref in sums[1:]:
        shrunk += ref[...]
    rows, held = out_ref.shape[0], slot_ref.shape[1]
    shrunk = jnp.transpose(jnp.concatenate([shrunk] * (held // rank), axis=0))
    slot = slot_ref[:rows]
    update = 0.0
    at = 0
    for i, depth in enumerate(groups):
        spread = jnp.concatenate(
            [
                jnp.where(slot[:, :lanes] == slots_ref[:, at + j : at + j + lanes], shrunk[:, :lanes], 0.0)
                for j in range(0, depth, held)
                for lanes in [min(held, depth - j)]
            ],
            axis=1,
        )
        at += depth
        high = spread.astype(jnp.bfloat16)
        low = (spread - high.astype(jnp.float32)).astype(jnp.bfloat16)
        for left, right in ((high, parts[2 * i]), (low, parts[2 * i]), (high, parts[2 * i + 1])):
            update += jnp.dot(left, right[...], preferred_element_type=jnp.float32)
    total = scale * update
    for base in bases:
        total += base[...]
    out_ref[...] = total.astype(jnp.bfloat16)


def expand_step(slots, slot, shrunk, parts, bases, rank, scale):
    groups = [high.shape[0] for high, _ in parts]
    flat = [term for pair in parts for term in pair]
    operands = [slots, slot, *flat, *bases, *shrunk]
    vmem = pl.BlockSpec(memory_space=pltpu.VMEM)
    return pl.pallas_call(
        lambda *refs: expand_kernel(rank, groups, scale, len(shrunk), *refs),
        in_specs=[vmem] * len(operands),
        out_specs=vmem,
        out_shape=jax.ShapeDtypeStruct(bases[0].shape, jnp.bfloat16),
        compiler_params=pltpu.CompilerParams(vmem_limit_bytes=16 * 2**20),
        cost_estimate=pl.CostEstimate(flops=0, bytes_accessed=0, transcendentals=0),
        name="expand_step",
    )(*operands)


def per_device(tokens, token_adapter_index, table, value_matrix, shrink_weight, expand_weight):
    rows, width = tokens.shape
    resident, rank, span = expand_weight.shape
    held = resident * rank
    owners = lax.axis_size("adapter")
    spots = owners // 2
    quarter = width // 4
    g, a = lax.axis_index("group"), lax.axis_index("adapter")
    c, half = a % 2, a // 2
    core_pairs = [(i, i ^ 1) for i in range(owners)]
    swap = [(0, 1), (1, 0)]
    barrier = lax.optimization_barrier

    def over_core(value):
        return lax.ppermute(value, "adapter", core_pairs)

    def over_group(value):
        return lax.ppermute(value, "group", swap)

    def shrink_rows(weight, side):
        rows_there = lax.dynamic_slice_in_dim(weight, (2 * g + side) * quarter, quarter, 0)
        return (rows_there * SHRINK_GAIN).astype(jnp.float16)

    half_expand = lax.dynamic_slice_in_dim(
        expand_weight.reshape(held, span), g * (held // 2), held // 2, 0
    )
    half_expand = (half_expand * EXPAND_GAIN).astype(jnp.float16)
    blocks = [half_expand[:, i * LANES : (i + 1) * LANES] for i in range(span // LANES)]
    mine = jnp.concatenate([shrink_rows(shrink_weight, c), *blocks], axis=0)
    four = spots == 4
    if four:
        mine_line = FourLine(mine, half)
        mine_line.first()
    else:
        mine_line = Line(mine, spots, half)
        mine_line.advance()

    later_weight, _ = barrier((shrink_weight, mine))
    given = over_core(shrink_rows(later_weight, 1 - c))
    if four:
        given_line = FourLine(given, half)
        given_line.first()
    else:
        given_line = Line(given, spots, half)
        given_line.advance()

    later, _ = barrier((tokens, given))
    places = [2 * (1 - g) + 1 - c, 2 * (1 - g) + c, 2 * g + 1 - c]
    slot, sent, kept = pack(later, table, token_adapter_index[None, :], places, quarter)
    theirs = over_group(sent)
    came_theirs = over_core(theirs[: rows + PAD])

    source = jnp.asarray(sources(spots))[half]
    firsts = resident * (2 * source[:, None] + jnp.stack([c, 1 - c])[None, :]).reshape(-1)
    axes = ("tensor", "sub")
    two = lax.axis_size("tensor") == 2 and lax.axis_size("sub") == 1
    x = lax.axis_index("tensor")
    if four and two:
        tokens_1, mine_line.end, mine_line.middle = barrier((tokens, mine_line.end, mine_line.middle))
        mine_line.second()
        (away,) = base_product(tokens_1, value_matrix, [1 - x], span)
        given_line.end, given_line.middle, away = barrier((given_line.end, given_line.middle, away))
        given_line.second()
        tokens_2, _ = barrier((tokens, given_line.end))
        (own_base,) = base_product(tokens_2, value_matrix, [x], span)
        mine_line.far_middle, own_base = barrier((mine_line.far_middle, own_base))
        mine_line.far_end, kept = barrier((mine_line.far_end, kept))
        given_line.far_middle, away = barrier((given_line.far_middle, away))
        bases = [own_base, lax.ppermute(away, "tensor", swap)]
    elif two:
        away, own_base = base_product(tokens, value_matrix, [1 - x, x], span)
        bases = [own_base, lax.ppermute(away, "tensor", swap)]
    else:
        if four:
            mine_line.second()
            given_line.second()
        partial = jnp.dot(tokens, value_matrix, preferred_element_type=jnp.float32)
        bases = [lax.psum_scatter(partial, axes, scatter_dimension=1, tiled=True)]
    came_own = over_core(kept)

    if four:
        mine_line.third()
        given_line.third()
    else:
        for _ in range(spots - 2):
            mine_line.advance()
            given_line.advance()
    mine_pieces, given_pieces = mine_line.pieces(), given_line.pieces()

    column = (2 * g + c) * quarter

    def weights_of(start, stop):
        weights = []
        for i in range(start, stop):
            weights += [side_by_side(mine_pieces[i][:quarter]), side_by_side(given_pieces[i])]
        return weights

    def products(operands, places, weights, start, sums=(), slots=(), mode=0):
        which = list(range(start, start + len(weights)))
        return shrink_step(
            operands, places, weights, firsts, column, which, sums, slots, mode, rows, rank, resident
        )

    here_parts = ((tokens, slot, came_own), ((0, 0, 1), (2, 0, None)))
    there_parts = ((theirs, came_theirs), ((0, rows + PAD, None), (1, 0, None)))
    all_parts = (
        (tokens, slot, came_own, theirs, came_theirs),
        ((0, 0, 1), (2, 0, None), (3, rows + PAD, None), (4, 0, None)),
    )
    last = len(mine_pieces) - 1
    some = min(3, last)
    here_sum, here_slot = products(*here_parts, weights_of(0, some), 0)
    there_sum, there_slot = products(*there_parts, weights_of(0, some), 0)
    late_mine, late_given = mine_pieces, given_pieces
    if four:
        mine_line.last, here_sum = barrier((mine_line.last, here_sum))
        mine_pieces = mine_line.pieces()
        mine_line.last, given_line.last, here_sum, there_sum = barrier(
            (mine_line.last, given_line.last, here_sum, there_sum)
        )
        late_mine, late_given = mine_line.pieces(), given_line.pieces()
    sums, slots_of = (here_sum, there_sum), (here_slot, there_slot)
    for start in range(some, last, 3):
        weights = weights_of(start, min(start + 3, last))
        sums = products(*all_parts, weights, 2 * start, sums, slots_of, 1)
    sums = products(*all_parts, [side_by_side(late_mine[last][:quarter])], 2 * last, sums, slots_of, 1)
    (almost,) = sums
    if four:
        given_line.last, almost = barrier((given_line.last, almost))
        late_given = given_line.pieces()
    stays, leaves = products(
        *all_parts, [side_by_side(late_given[last])], 2 * last + 1, (almost,), slots_of, 2
    )
    both_sum = stays + over_core(leaves)
    own_sum, other_sum = both_sum[:, :rows], both_sum[:, rows:]
    if len(bases) == 2:
        across = [(i, 3 - i) for i in range(4)]
        shrunk = [
            own_sum,
            lax.ppermute(other_sum, ("group", "tensor"), across),
            over_group(other_sum),
            lax.ppermute(own_sum, "tensor", swap),
        ]
    else:
        shrunk = [lax.psum(own_sum + over_group(other_sum), axes)]

    def expand_of(piece):
        cut = piece[quarter:].reshape(span // LANES, held // 2, LANES)
        return jnp.concatenate([cut[i] for i in range(span // LANES)], axis=1)

    here = jnp.concatenate([expand_of(piece) for piece in mine_pieces], axis=0)
    across, _ = barrier((over_group(here), both_sum))
    beside = over_core(jnp.concatenate([here, across], axis=0))
    terms = [two_terms(here), two_terms(across), two_terms(beside)]
    steps = jnp.arange(resident // 2, dtype=jnp.int32)
    sides = jnp.stack([c, 1 - c])[:, None, None, None]
    halves = jnp.stack([g, 1 - g])[None, :, None, None] * (resident // 2)
    slots = (2 * source[:, None] + sides) * resident + halves + steps
    slots = jnp.repeat(slots.astype(jnp.int32).reshape(1, -1), rank, axis=1)
    scale = SCALING / (SHRINK_GAIN * EXPAND_GAIN)
    return expand_step(slots, here_slot, shrunk, terms, bases, rank, scale)


def solution(mesh):
    placed = (
        P(("group", "adapter"), ("tensor", "sub")),
        P(("group", "adapter")),
        P("group"),
        P(("tensor", "sub"), None),
        P(("tensor", "sub"), "adapter"),
        P("adapter", None, ("tensor", "sub")),
    )
    return jax.shard_map(
        per_device,
        mesh=mesh,
        in_specs=placed,
        out_specs=P(("group", "adapter"), ("tensor", "sub")),
        check_vma=False,
    )
```

```python
import jax
import jax.numpy as jnp
import numpy as np
from jax import lax
from jax.experimental import pallas as pl
from jax.experimental.pallas import tpu as pltpu
from jax.sharding import PartitionSpec as P

SCALING = 0.5
SHRINK_GAIN = 2.0**19
EXPAND_GAIN = 2.0**14
LANES = 128


def sources(spots):
    if spots == 4:
        return np.array([[0, 1, 2, 3], [1, 0, 2, 3], [2, 3, 1, 0], [3, 2, 1, 0]], np.int32)
    table = []
    for half in range(spots):
        found = [half]
        for step in range(1, spots):
            up, down = half - step, half + step
            if 2 * step > spots - 1:
                found.append(up if half >= step else down)
            else:
                found += [up, down]
        table.append([f if 0 <= f < spots else -(2**16) for f in found])
    return np.array(table, np.int32)


class FourLine:
    def __init__(self, piece, half):
        self.own, self.half = piece, half

    def send(self, value, moves):
        return lax.ppermute(value, "adapter", [(2 * s + c, 2 * d + c) for s, d in moves for c in range(2)])

    def first(self):
        self.end = self.send(self.own, [(0, 1), (1, 0), (2, 3), (3, 2)])
        self.middle = self.send(self.own, [(1, 2), (2, 1)])

    def second(self):
        self.far_middle = self.send(self.end, [(1, 2), (2, 1)])
        self.far_end = self.send(self.middle, [(1, 0), (2, 3)])

    def third(self):
        self.last = self.send(self.far_middle, [(1, 0), (2, 3)])

    def pieces(self):
        inner = (self.half == 1) | (self.half == 2)
        return [
            self.own,
            self.end,
            jnp.where(inner, self.middle, self.far_end),
            jnp.where(inner, self.far_middle, self.last),
        ]


class Line:
    def __init__(self, piece, spots, half):
        self.spots, self.half = spots, half
        self.up = self.down = piece
        self.found, self.step = [piece], 1

    def send(self, value, moves):
        return lax.ppermute(value, "adapter", [(2 * s + c, 2 * d + c) for s, d in moves for c in range(2)])

    def advance(self):
        spots, step, half = self.spots, self.step, self.half
        goes_up = [(s, s + 1) for s in range(step - 1, spots - 1)]
        goes_down = [(s, s - 1) for s in range(1, spots - step + 1)]
        self.step += 1
        if 2 * step - 1 > spots:
            self.up = self.down = self.send(self.up, goes_up + goes_down)
            self.found.append(self.up)
            return
        self.up, self.down = self.send(self.up, goes_up), self.send(self.down, goes_down)
        if 2 * step > spots - 1:
            self.up = self.down = jnp.where(half >= step, self.up, self.down)
            self.found.append(self.up)
        else:
            self.found += [self.up, self.down]

    def pieces(self):
        return self.found


def two_terms(value):
    wide = value.astype(jnp.float32)
    high = lax.reduce_precision(wide, exponent_bits=8, mantissa_bits=7)
    return high.astype(jnp.bfloat16), (wide - high).astype(jnp.bfloat16)


def side_by_side(value):
    return jnp.concatenate(two_terms(value), axis=1)


def product_kernel(span, pieces, place_ref, tokens_ref, matrix_ref, *refs):
    out_refs, (tokens_here, matrix_here, token_sems, matrix_sems) = refs[:-4], refs[-4:]
    depth = tokens_ref.shape[1] // pieces
    parts = [pl.ds(k * depth, depth) for k in range(pieces)]
    copies = [[] for _ in out_refs]
    for i in range(len(out_refs)):
        columns = pl.ds(pl.multiple_of(place_ref[i] * span, LANES), span)
        for k, part in enumerate(parts):
            arriving = []
            if i == 0:
                arriving.append(
                    pltpu.make_async_copy(
                        tokens_ref.at[:, part], tokens_here.at[:, part], token_sems.at[k]
                    )
                )
            arriving.append(
                pltpu.make_async_copy(
                    matrix_ref.at[part, columns], matrix_here.at[i, part], matrix_sems.at[i, k]
                )
            )
            for copy in arriving:
                copy.start()
            copies[i].append(arriving)
    for i, out_ref in enumerate(out_refs):
        total = 0.0
        for k, part in enumerate(parts):
            for copy in copies[i][k]:
                copy.wait()
            total += jnp.dot(
                tokens_here[:, part], matrix_here[i, part], preferred_element_type=jnp.float32
            )
        out_ref[...] = total


def base_product(tokens, matrix, places, span):
    rows, width = tokens.shape
    pieces = 4
    vmem, hbm = pl.BlockSpec(memory_space=pltpu.VMEM), pl.BlockSpec(memory_space=pltpu.HBM)
    return pl.pallas_call(
        lambda *refs: product_kernel(span, pieces, *refs),
        in_specs=[pl.BlockSpec(memory_space=pltpu.SMEM), hbm, hbm],
        out_specs=[vmem] * len(places),
        out_shape=[jax.ShapeDtypeStruct((rows, span), jnp.float32)] * len(places),
        scratch_shapes=[
            pltpu.VMEM((rows, width), tokens.dtype),
            pltpu.VMEM((len(places), width, span), matrix.dtype),
            pltpu.SemaphoreType.DMA((pieces,)),
            pltpu.SemaphoreType.DMA((len(places), pieces)),
        ],
        compiler_params=pltpu.CompilerParams(vmem_limit_bytes=52 * 2**20),
        cost_estimate=pl.CostEstimate(flops=0, bytes_accessed=0, transcendentals=0),
        name="base_product",
    )(jnp.stack(places), tokens, matrix)


def lay_out_kernel(shrink_at_ref, expand_at_ref, shrink_ref, expand_ref, out_ref, sems):
    count = expand_ref.shape[0] // 2
    blocks = expand_ref.shape[1] // LANES
    quarter = out_ref.shape[0] - blocks * count
    rows = pl.ds(pl.multiple_of(shrink_at_ref[0] * quarter, 8), quarter)
    copies = [pltpu.make_async_copy(shrink_ref.at[rows], out_ref.at[pl.ds(0, quarter)], sems.at[0])]
    held = pl.ds(pl.multiple_of(expand_at_ref[0] * count, 8), count)
    for i in range(blocks):
        copies.append(
            pltpu.make_async_copy(
                expand_ref.at[held, pl.ds(i * LANES, LANES)],
                out_ref.at[pl.ds(quarter + i * count, count)],
                sems.at[i + 1],
            )
        )
    for copy in copies:
        copy.start()
    for copy in copies:
        copy.wait()


def lay_out(shrink, expand, shrink_at, expand_at, quarter):
    held, span = expand.shape
    smem, hbm = pl.BlockSpec(memory_space=pltpu.SMEM), pl.BlockSpec(memory_space=pltpu.HBM)
    rows = quarter + held // 2 * (span // LANES)
    return pl.pallas_call(
        lay_out_kernel,
        in_specs=[smem, smem, hbm, hbm],
        out_specs=pl.BlockSpec(memory_space=pltpu.VMEM),
        out_shape=jax.ShapeDtypeStruct((rows, LANES), jnp.float32),
        scratch_shapes=[pltpu.SemaphoreType.DMA((span // LANES + 1,))],
        compiler_params=pltpu.CompilerParams(vmem_limit_bytes=16 * 2**20),
        cost_estimate=pl.CostEstimate(flops=0, bytes_accessed=0, transcendentals=0),
        name="lay_out",
    )(jnp.reshape(shrink_at, (1,)), jnp.reshape(expand_at, (1,)), shrink, expand)


PAD = 16


def pack_kernel(rows, quarter, *refs):
    column_refs, (table_ref, index_ref, tokens_ref, slot_ref, sent_ref, kept_ref, sems) = refs[:3], refs[3:]
    step = rows + PAD
    places = ((sent_ref, 0), (sent_ref, step), (kept_ref, 0))
    copies = []
    for i, (out_ref, start) in enumerate(places):
        column = pl.multiple_of(column_refs[i][0] * quarter, LANES)
        copies.append(
            pltpu.make_async_copy(
                tokens_ref.at[:, pl.ds(column, quarter)], out_ref.at[pl.ds(start, rows)], sems.at[i]
            )
        )
        copies[i].start()
    index = index_ref[...]
    slot = jnp.zeros_like(index)
    for j in range(table_ref.shape[0]):
        slot += jnp.where(index == j, table_ref[j], 0)
    slot_ref[...] = slot
    tail = jnp.broadcast_to(slot.astype(jnp.float32), (PAD, rows)).astype(sent_ref.dtype)
    for out_ref, start in places:
        out_ref[start + rows : start + step, :rows] = tail
        if quarter > rows:
            out_ref[start + rows : start + step, rows:] = jnp.zeros((PAD, quarter - rows), out_ref.dtype)
    for copy in copies:
        copy.wait()


def pack(tokens, table, index, places, quarter):
    rows = tokens.shape[0]
    vmem, smem = pl.BlockSpec(memory_space=pltpu.VMEM), pl.BlockSpec(memory_space=pltpu.SMEM)
    return pl.pallas_call(
        lambda *refs: pack_kernel(rows, quarter, *refs),
        in_specs=[smem] * 4 + [vmem, pl.BlockSpec(memory_space=pltpu.HBM)],
        out_specs=[vmem] * 3,
        out_shape=[
            jax.ShapeDtypeStruct((1, rows), jnp.int32),
            jax.ShapeDtypeStruct((2 * (rows + PAD), quarter), tokens.dtype),
            jax.ShapeDtypeStruct((rows + PAD, quarter), tokens.dtype),
        ],
        scratch_shapes=[pltpu.SemaphoreType.DMA((3,))],
        compiler_params=pltpu.CompilerParams(vmem_limit_bytes=16 * 2**20),
        cost_estimate=pl.CostEstimate(flops=0, bytes_accessed=0, transcendentals=0),
        name="pack",
    )(*[jnp.reshape(place, (1,)) for place in places], table, index, tokens)


def shrink_kernel(rank, resident, rows, which, places, mode, first_ref, column_ref, *refs):
    held = rank * resident
    count = 1 + max(max(p[0], p[2] or 0) for p in places)
    operands, refs = refs[:count], refs[count:]
    weights, refs = refs[: len(which)], refs[len(which) :]
    quarter = weights[0].shape[0]
    group = lax.broadcasted_iota(jnp.int32, (1, held), 1) // rank

    def rows_of(arrays, part):
        per = arrays[0].shape[0] // rows
        return arrays[part // per][part % per * rows : (part % per + 1) * rows]

    if mode:
        outs = refs[-mode:]
        inputs = refs[:-mode]
        slot_rows = inputs[-(len(places) // 2) :]
        sums = inputs[: -(len(places) // 2)]
    for part, (operand, row, slots) in enumerate(places):
        if slots is None:
            tokens = operands[operand][row : row + rows]
        else:
            tokens = operands[operand][:, pl.ds(pl.multiple_of(column_ref[0], quarter), quarter)]
        if mode:
            slot = rows_of(slot_rows, part)
            total = rows_of(sums, part)
        else:
            if slots is None:
                slot = operands[operand][row + rows : row + rows + PAD, :rows].astype(jnp.float32)[:1]
            else:
                slot = operands[slots][...].astype(jnp.float32)
            slot = jnp.transpose(jnp.broadcast_to(slot, (held, rows))).astype(jnp.int32)
            refs[1][part * rows : (part + 1) * rows] = slot
            total = jnp.zeros((rows, held), jnp.float32)
        for w, side in zip(weights, which):
            product = jnp.dot(tokens, w[...], preferred_element_type=jnp.float32)
            chosen = slot == first_ref[side] + group
            total = jnp.where(chosen, product[:, :held] + product[:, held:], total)
        if mode < 2:
            out_ref = outs[0] if mode else refs[0]
            out_ref[part * rows : (part + 1) * rows] = total
        else:
            total = jnp.transpose(total)
            gathered = total[:rank]
            for j in range(1, resident):
                gathered += total[j * rank : (j + 1) * rank]
            at = part // 2 * rows
            outs[part % 2][:, at : at + rows] = gathered


def shrink_step(operands, places, weights, firsts, column, which, sums, slots, mode, rows, rank, resident):
    vmem = pl.BlockSpec(memory_space=pltpu.VMEM)
    smem = pl.BlockSpec(memory_space=pltpu.SMEM)
    operands = [*operands, *weights, *sums, *slots]
    count, held = len(places) * rows, rank * resident
    wide = jax.ShapeDtypeStruct((count, held), jnp.float32)
    narrow = jax.ShapeDtypeStruct((rank, count // 2), jnp.float32)
    shapes = [[wide, jax.ShapeDtypeStruct((count, held), jnp.int32)], [wide], [narrow, narrow]][mode]
    return pl.pallas_call(
        lambda *refs: shrink_kernel(rank, resident, rows, which, places, mode, *refs),
        in_specs=[smem, smem] + [vmem] * len(operands),
        out_specs=[vmem] * len(shapes),
        out_shape=shapes,
        compiler_params=pltpu.CompilerParams(vmem_limit_bytes=16 * 2**20),
        cost_estimate=pl.CostEstimate(flops=0, bytes_accessed=0, transcendentals=0),
        name="shrink_step",
    )(firsts, jnp.reshape(column, (1,)), *operands)


def expand_kernel(rank, groups, scale, count, slots_ref, slot_ref, *refs):
    parts = refs[: 2 * len(groups)]
    bases, sums, out_ref = refs[2 * len(groups) : -1 - count], refs[-1 - count : -1], refs[-1]
    shrunk = sums[0][...]
    for ref in sums[1:]:
        shrunk += ref[...]
    rows, held = out_ref.shape[0], slot_ref.shape[1]
    shrunk = jnp.transpose(jnp.concatenate([shrunk] * (held // rank), axis=0))
    slot = slot_ref[:rows]
    update = 0.0
    at = 0
    for i, depth in enumerate(groups):
        spread = jnp.concatenate(
            [
                jnp.where(slot[:, :lanes] == slots_ref[:, at + j : at + j + lanes], shrunk[:, :lanes], 0.0)
                for j in range(0, depth, held)
                for lanes in [min(held, depth - j)]
            ],
            axis=1,
        )
        at += depth
        high = spread.astype(jnp.bfloat16)
        low = (spread - high.astype(jnp.float32)).astype(jnp.bfloat16)
        for left, right in ((high, parts[2 * i]), (low, parts[2 * i]), (high, parts[2 * i + 1])):
            update += jnp.dot(left, right[...], preferred_element_type=jnp.float32)
    total = scale * update
    for base in bases:
        total += base[...]
    out_ref[...] = total.astype(jnp.bfloat16)


def expand_step(slots, slot, shrunk, parts, bases, rank, scale):
    groups = [high.shape[0] for high, _ in parts]
    flat = [term for pair in parts for term in pair]
    operands = [slots, slot, *flat, *bases, *shrunk]
    vmem = pl.BlockSpec(memory_space=pltpu.VMEM)
    return pl.pallas_call(
        lambda *refs: expand_kernel(rank, groups, scale, len(shrunk), *refs),
        in_specs=[vmem] * len(operands),
        out_specs=vmem,
        out_shape=jax.ShapeDtypeStruct(bases[0].shape, jnp.bfloat16),
        compiler_params=pltpu.CompilerParams(vmem_limit_bytes=16 * 2**20),
        cost_estimate=pl.CostEstimate(flops=0, bytes_accessed=0, transcendentals=0),
        name="expand_step",
    )(*operands)


def per_device(tokens, token_adapter_index, table, value_matrix, shrink_weight, expand_weight):
    rows, width = tokens.shape
    resident, rank, span = expand_weight.shape
    held = resident * rank
    owners = lax.axis_size("adapter")
    spots = owners // 2
    quarter = width // 4
    g, a = lax.axis_index("group"), lax.axis_index("adapter")
    c, half = a % 2, a // 2
    core_pairs = [(i, i ^ 1) for i in range(owners)]
    swap = [(0, 1), (1, 0)]
    barrier = lax.optimization_barrier

    def over_core(value):
        return lax.ppermute(value, "adapter", core_pairs)

    def over_group(value):
        return lax.ppermute(value, "group", swap)

    def shrink_rows(weight, side):
        rows_there = lax.dynamic_slice_in_dim(weight, (2 * g + side) * quarter, quarter, 0)
        return (rows_there * SHRINK_GAIN).astype(jnp.float16)

    laid = lay_out(shrink_weight, expand_weight.reshape(held, span), 2 * g + c, g, quarter)
    is_shrink = lax.broadcasted_iota(jnp.int32, laid.shape, 0) < quarter
    mine = (laid * jnp.where(is_shrink, SHRINK_GAIN, EXPAND_GAIN)).astype(jnp.float16)
    four = spots == 4
    if four:
        mine_line = FourLine(mine, half)
        mine_line.first()
    else:
        mine_line = Line(mine, spots, half)
        mine_line.advance()

    later_weight, _ = barrier((shrink_weight, mine))
    given = over_core(shrink_rows(later_weight, 1 - c))
    if four:
        given_line = FourLine(given, half)
        given_line.first()
    else:
        given_line = Line(given, spots, half)
        given_line.advance()

    later, _ = barrier((tokens, given))
    places = [2 * (1 - g) + 1 - c, 2 * (1 - g) + c, 2 * g + 1 - c]
    slot, sent, kept = pack(later, table, token_adapter_index[None, :], places, quarter)
    theirs = over_group(sent)
    came_theirs = over_core(theirs[: rows + PAD])

    source = jnp.asarray(sources(spots))[half]
    firsts = resident * (2 * source[:, None] + jnp.stack([c, 1 - c])[None, :]).reshape(-1)
    axes = ("tensor", "sub")
    two = lax.axis_size("tensor") == 2 and lax.axis_size("sub") == 1
    x = lax.axis_index("tensor")
    if four and two:
        tokens_1, mine_line.end, mine_line.middle = barrier((tokens, mine_line.end, mine_line.middle))
        mine_line.second()
        (away,) = base_product(tokens_1, value_matrix, [1 - x], span)
        given_line.end, given_line.middle, away = barrier((given_line.end, given_line.middle, away))
        given_line.second()
        tokens_2, _ = barrier((tokens, given_line.end))
        (own_base,) = base_product(tokens_2, value_matrix, [x], span)
        mine_line.far_middle, own_base = barrier((mine_line.far_middle, own_base))
        mine_line.far_end, kept = barrier((mine_line.far_end, kept))
        given_line.far_middle, away = barrier((given_line.far_middle, away))
        bases = [own_base, lax.ppermute(away, "tensor", swap)]
    elif two:
        away, own_base = base_product(tokens, value_matrix, [1 - x, x], span)
        bases = [own_base, lax.ppermute(away, "tensor", swap)]
    else:
        if four:
            mine_line.second()
            given_line.second()
        partial = jnp.dot(tokens, value_matrix, preferred_element_type=jnp.float32)
        bases = [lax.psum_scatter(partial, axes, scatter_dimension=1, tiled=True)]
    came_own = over_core(kept)

    if four:
        mine_line.third()
        given_line.third()
    else:
        for _ in range(spots - 2):
            mine_line.advance()
            given_line.advance()
    mine_pieces, given_pieces = mine_line.pieces(), given_line.pieces()

    column = (2 * g + c) * quarter

    def weights_of(start, stop):
        weights = []
        for i in range(start, stop):
            weights += [side_by_side(mine_pieces[i][:quarter]), side_by_side(given_pieces[i])]
        return weights

    def products(operands, places, weights, start, sums=(), slots=(), mode=0):
        which = list(range(start, start + len(weights)))
        return shrink_step(
            operands, places, weights, firsts, column, which, sums, slots, mode, rows, rank, resident
        )

    here_parts = ((tokens, slot, came_own), ((0, 0, 1), (2, 0, None)))
    there_parts = ((theirs, came_theirs), ((0, rows + PAD, None), (1, 0, None)))
    all_parts = (
        (tokens, slot, came_own, theirs, came_theirs),
        ((0, 0, 1), (2, 0, None), (3, rows + PAD, None), (4, 0, None)),
    )
    last = len(mine_pieces) - 1
    some = min(3, last)
    here_sum, here_slot = products(*here_parts, weights_of(0, some), 0)
    there_sum, there_slot = products(*there_parts, weights_of(0, some), 0)
    late_mine, late_given = mine_pieces, given_pieces
    if four:
        mine_line.last, here_sum = barrier((mine_line.last, here_sum))
        mine_pieces = mine_line.pieces()
        mine_line.last, given_line.last, here_sum, there_sum = barrier(
            (mine_line.last, given_line.last, here_sum, there_sum)
        )
        late_mine, late_given = mine_line.pieces(), given_line.pieces()
    sums, slots_of = (here_sum, there_sum), (here_slot, there_slot)
    for start in range(some, last, 3):
        weights = weights_of(start, min(start + 3, last))
        sums = products(*all_parts, weights, 2 * start, sums, slots_of, 1)
    sums = products(*all_parts, [side_by_side(late_mine[last][:quarter])], 2 * last, sums, slots_of, 1)
    (almost,) = sums
    if four:
        given_line.last, almost = barrier((given_line.last, almost))
        late_given = given_line.pieces()
    stays, leaves = products(
        *all_parts, [side_by_side(late_given[last])], 2 * last + 1, (almost,), slots_of, 2
    )
    both_sum = stays + over_core(leaves)
    own_sum, other_sum = both_sum[:, :rows], both_sum[:, rows:]
    if len(bases) == 2:
        across = [(i, 3 - i) for i in range(4)]
        shrunk = [
            own_sum,
            lax.ppermute(other_sum, ("group", "tensor"), across),
            over_group(other_sum),
            lax.ppermute(own_sum, "tensor", swap),
        ]
    else:
        shrunk = [lax.psum(own_sum + over_group(other_sum), axes)]

    def expand_of(piece):
        cut = piece[quarter:].reshape(span // LANES, held // 2, LANES)
        return jnp.concatenate([cut[i] for i in range(span // LANES)], axis=1)

    here = jnp.concatenate([expand_of(piece) for piece in mine_pieces], axis=0)
    across, _ = barrier((over_group(here), both_sum))
    beside = over_core(jnp.concatenate([here, across], axis=0))
    terms = [two_terms(here), two_terms(across), two_terms(beside)]
    steps = jnp.arange(resident // 2, dtype=jnp.int32)
    sides = jnp.stack([c, 1 - c])[:, None, None, None]
    halves = jnp.stack([g, 1 - g])[None, :, None, None] * (resident // 2)
    slots = (2 * source[:, None] + sides) * resident + halves + steps
    slots = jnp.repeat(slots.astype(jnp.int32).reshape(1, -1), rank, axis=1)
    scale = SCALING / (SHRINK_GAIN * EXPAND_GAIN)
    return expand_step(slots, here_slot, shrunk, terms, bases, rank, scale)


def solution(mesh):
    placed = (
        P(("group", "adapter"), ("tensor", "sub")),
        P(("group", "adapter")),
        P("group"),
        P(("tensor", "sub"), None),
        P(("tensor", "sub"), "adapter"),
        P("adapter", None, ("tensor", "sub")),
    )
    return jax.shard_map(
        per_device,
        mesh=mesh,
        in_specs=placed,
        out_specs=P(("group", "adapter"), ("tensor", "sub")),
        check_vma=False,
    )
```

```python
import jax
import jax.numpy as jnp
import numpy as np
from jax import lax
from jax.experimental import pallas as pl
from jax.experimental.pallas import tpu as pltpu
from jax.sharding import PartitionSpec as P

SCALING = 0.5
SHRINK_GAIN = 2.0**19
EXPAND_GAIN = 2.0**14
LANES = 128


def sources(spots):
    if spots == 4:
        return np.array([[0, 1, 2, 3], [1, 0, 2, 3], [2, 3, 1, 0], [3, 2, 1, 0]], np.int32)
    table = []
    for half in range(spots):
        found = [half]
        for step in range(1, spots):
            up, down = half - step, half + step
            if 2 * step > spots - 1:
                found.append(up if half >= step else down)
            else:
                found += [up, down]
        table.append([f if 0 <= f < spots else -(2**16) for f in found])
    return np.array(table, np.int32)


class FourLine:
    def __init__(self, piece, half):
        self.own, self.half = piece, half

    def send(self, value, moves):
        return lax.ppermute(value, "adapter", [(2 * s + c, 2 * d + c) for s, d in moves for c in range(2)])

    def first(self):
        self.end = self.send(self.own, [(0, 1), (1, 0), (2, 3), (3, 2)])
        self.middle = self.send(self.own, [(1, 2), (2, 1)])

    def second(self):
        self.far_middle = self.send(self.end, [(1, 2), (2, 1)])
        self.far_end = self.send(self.middle, [(1, 0), (2, 3)])

    def third(self):
        self.last = self.send(self.far_middle, [(1, 0), (2, 3)])

    def pieces(self):
        inner = (self.half == 1) | (self.half == 2)
        return [
            self.own,
            self.end,
            jnp.where(inner, self.middle, self.far_end),
            jnp.where(inner, self.far_middle, self.last),
        ]


class Line:
    def __init__(self, piece, spots, half):
        self.spots, self.half = spots, half
        self.up = self.down = piece
        self.found, self.step = [piece], 1

    def send(self, value, moves):
        return lax.ppermute(value, "adapter", [(2 * s + c, 2 * d + c) for s, d in moves for c in range(2)])

    def advance(self):
        spots, step, half = self.spots, self.step, self.half
        goes_up = [(s, s + 1) for s in range(step - 1, spots - 1)]
        goes_down = [(s, s - 1) for s in range(1, spots - step + 1)]
        self.step += 1
        if 2 * step - 1 > spots:
            self.up = self.down = self.send(self.up, goes_up + goes_down)
            self.found.append(self.up)
            return
        self.up, self.down = self.send(self.up, goes_up), self.send(self.down, goes_down)
        if 2 * step > spots - 1:
            self.up = self.down = jnp.where(half >= step, self.up, self.down)
            self.found.append(self.up)
        else:
            self.found += [self.up, self.down]

    def pieces(self):
        return self.found


def two_terms(value):
    wide = value.astype(jnp.float32)
    high = lax.reduce_precision(wide, exponent_bits=8, mantissa_bits=7)
    return high.astype(jnp.bfloat16), (wide - high).astype(jnp.bfloat16)


def side_by_side(value):
    return jnp.concatenate(two_terms(value), axis=1)


def product_kernel(span, pieces, place_ref, tokens_ref, matrix_ref, *refs):
    out_refs, (tokens_here, matrix_here, token_sems, matrix_sems) = refs[:-4], refs[-4:]
    depth = tokens_ref.shape[1] // pieces
    parts = [pl.ds(k * depth, depth) for k in range(pieces)]
    copies = [[] for _ in out_refs]
    for i in range(len(out_refs)):
        columns = pl.ds(pl.multiple_of(place_ref[i] * span, LANES), span)
        for k, part in enumerate(parts):
            arriving = []
            if i == 0:
                arriving.append(
                    pltpu.make_async_copy(
                        tokens_ref.at[:, part], tokens_here.at[:, part], token_sems.at[k]
                    )
                )
            arriving.append(
                pltpu.make_async_copy(
                    matrix_ref.at[part, columns], matrix_here.at[i, part], matrix_sems.at[i, k]
                )
            )
            for copy in arriving:
                copy.start()
            copies[i].append(arriving)
    for i, out_ref in enumerate(out_refs):
        total = 0.0
        for k, part in enumerate(parts):
            for copy in copies[i][k]:
                copy.wait()
            total += jnp.dot(
                tokens_here[:, part], matrix_here[i, part], preferred_element_type=jnp.float32
            )
        out_ref[...] = total


def base_product(tokens, matrix, places, span):
    rows, width = tokens.shape
    pieces = 4
    vmem, hbm = pl.BlockSpec(memory_space=pltpu.VMEM), pl.BlockSpec(memory_space=pltpu.HBM)
    return pl.pallas_call(
        lambda *refs: product_kernel(span, pieces, *refs),
        in_specs=[pl.BlockSpec(memory_space=pltpu.SMEM), hbm, hbm],
        out_specs=[vmem] * len(places),
        out_shape=[jax.ShapeDtypeStruct((rows, span), jnp.float32)] * len(places),
        scratch_shapes=[
            pltpu.VMEM((rows, width), tokens.dtype),
            pltpu.VMEM((len(places), width, span), matrix.dtype),
            pltpu.SemaphoreType.DMA((pieces,)),
            pltpu.SemaphoreType.DMA((len(places), pieces)),
        ],
        compiler_params=pltpu.CompilerParams(vmem_limit_bytes=52 * 2**20),
        cost_estimate=pl.CostEstimate(flops=0, bytes_accessed=0, transcendentals=0),
        name="base_product",
    )(jnp.stack(places), tokens, matrix)


def lay_out_kernel(shrink_at_ref, expand_at_ref, shrink_ref, expand_ref, out_ref, sems):
    count = expand_ref.shape[0] // 2
    blocks = expand_ref.shape[1] // LANES
    quarter = out_ref.shape[0] - blocks * count
    rows = pl.ds(pl.multiple_of(shrink_at_ref[0] * quarter, 8), quarter)
    copies = [pltpu.make_async_copy(shrink_ref.at[rows], out_ref.at[pl.ds(0, quarter)], sems.at[0])]
    held = pl.ds(pl.multiple_of(expand_at_ref[0] * count, 8), count)
    for i in range(blocks):
        copies.append(
            pltpu.make_async_copy(
                expand_ref.at[held, pl.ds(i * LANES, LANES)],
                out_ref.at[pl.ds(quarter + i * count, count)],
                sems.at[i + 1],
            )
        )
    for copy in copies:
        copy.start()
    for copy in copies:
        copy.wait()


def lay_out(shrink, expand, shrink_at, expand_at, quarter):
    held, span = expand.shape
    smem, hbm = pl.BlockSpec(memory_space=pltpu.SMEM), pl.BlockSpec(memory_space=pltpu.HBM)
    rows = quarter + held // 2 * (span // LANES)
    return pl.pallas_call(
        lay_out_kernel,
        in_specs=[smem, smem, hbm, hbm],
        out_specs=pl.BlockSpec(memory_space=pltpu.VMEM),
        out_shape=jax.ShapeDtypeStruct((rows, LANES), jnp.float32),
        scratch_shapes=[pltpu.SemaphoreType.DMA((span // LANES + 1,))],
        compiler_params=pltpu.CompilerParams(vmem_limit_bytes=16 * 2**20),
        cost_estimate=pl.CostEstimate(flops=0, bytes_accessed=0, transcendentals=0),
        name="lay_out",
    )(jnp.reshape(shrink_at, (1,)), jnp.reshape(expand_at, (1,)), shrink, expand)


PAD = 16


def pack_kernel(rows, quarter, *refs):
    column_refs, (table_ref, index_ref, tokens_ref, slot_ref, sent_ref, kept_ref, sems) = refs[:3], refs[3:]
    step = rows + PAD
    places = ((sent_ref, 0), (sent_ref, step), (kept_ref, 0))
    copies = []
    for i, (out_ref, start) in enumerate(places):
        column = pl.multiple_of(column_refs[i][0] * quarter, LANES)
        copies.append(
            pltpu.make_async_copy(
                tokens_ref.at[:, pl.ds(column, quarter)], out_ref.at[pl.ds(start, rows)], sems.at[i]
            )
        )
        copies[i].start()
    index = index_ref[...]
    slot = jnp.zeros_like(index)
    for j in range(table_ref.shape[0]):
        slot += jnp.where(index == j, table_ref[j], 0)
    slot_ref[...] = slot
    tail = jnp.broadcast_to(slot.astype(jnp.float32), (PAD, rows)).astype(sent_ref.dtype)
    for out_ref, start in places:
        out_ref[start + rows : start + step, :rows] = tail
        if quarter > rows:
            out_ref[start + rows : start + step, rows:] = jnp.zeros((PAD, quarter - rows), out_ref.dtype)
    for copy in copies:
        copy.wait()


def pack(tokens, table, index, places, quarter):
    rows = tokens.shape[0]
    vmem, smem = pl.BlockSpec(memory_space=pltpu.VMEM), pl.BlockSpec(memory_space=pltpu.SMEM)
    return pl.pallas_call(
        lambda *refs: pack_kernel(rows, quarter, *refs),
        in_specs=[smem] * 4 + [vmem, pl.BlockSpec(memory_space=pltpu.HBM)],
        out_specs=[vmem] * 3,
        out_shape=[
            jax.ShapeDtypeStruct((1, rows), jnp.int32),
            jax.ShapeDtypeStruct((2 * (rows + PAD), quarter), tokens.dtype),
            jax.ShapeDtypeStruct((rows + PAD, quarter), tokens.dtype),
        ],
        scratch_shapes=[pltpu.SemaphoreType.DMA((3,))],
        compiler_params=pltpu.CompilerParams(vmem_limit_bytes=16 * 2**20),
        cost_estimate=pl.CostEstimate(flops=0, bytes_accessed=0, transcendentals=0),
        name="pack",
    )(*[jnp.reshape(place, (1,)) for place in places], table, index, tokens)


def shrink_kernel(rank, resident, rows, which, places, mode, first_ref, column_ref, *refs):
    held = rank * resident
    count = 1 + max(max(p[0], p[2] or 0) for p in places)
    operands, refs = refs[:count], refs[count:]
    weights, refs = refs[: len(which)], refs[len(which) :]
    quarter = weights[0].shape[0]
    group = lax.broadcasted_iota(jnp.int32, (1, held), 1) // rank

    def rows_of(arrays, part):
        per = arrays[0].shape[0] // rows
        return arrays[part // per][part % per * rows : (part % per + 1) * rows]

    if mode:
        outs = refs[-mode:]
        inputs = refs[:-mode]
        slot_rows = inputs[-(len(places) // 2) :]
        sums = inputs[: -(len(places) // 2)]
    for part, (operand, row, slots) in enumerate(places):
        if slots is None:
            tokens = operands[operand][row : row + rows]
        else:
            tokens = operands[operand][:, pl.ds(pl.multiple_of(column_ref[0], quarter), quarter)]
        if mode:
            slot = rows_of(slot_rows, part)
            total = rows_of(sums, part)
        else:
            if slots is None:
                slot = operands[operand][row + rows : row + rows + PAD, :rows].astype(jnp.float32)[:1]
            else:
                slot = operands[slots][...].astype(jnp.float32)
            slot = jnp.transpose(jnp.broadcast_to(slot, (held, rows))).astype(jnp.int32)
            refs[1][part * rows : (part + 1) * rows] = slot
            total = jnp.zeros((rows, held), jnp.float32)
        for w, side in zip(weights, which):
            product = jnp.dot(tokens, w[...], preferred_element_type=jnp.float32)
            chosen = slot == first_ref[side] + group
            total = jnp.where(chosen, product[:, :held] + product[:, held:], total)
        if mode < 2:
            out_ref = outs[0] if mode else refs[0]
            out_ref[part * rows : (part + 1) * rows] = total
        else:
            total = jnp.transpose(total)
            gathered = total[:rank]
            for j in range(1, resident):
                gathered += total[j * rank : (j + 1) * rank]
            at = part // 2 * rows
            outs[part % 2][:, at : at + rows] = gathered


def shrink_step(operands, places, weights, firsts, column, which, sums, slots, mode, rows, rank, resident):
    vmem = pl.BlockSpec(memory_space=pltpu.VMEM)
    smem = pl.BlockSpec(memory_space=pltpu.SMEM)
    operands = [*operands, *weights, *sums, *slots]
    count, held = len(places) * rows, rank * resident
    wide = jax.ShapeDtypeStruct((count, held), jnp.float32)
    narrow = jax.ShapeDtypeStruct((rank, count // 2), jnp.float32)
    shapes = [[wide, jax.ShapeDtypeStruct((count, held), jnp.int32)], [wide], [narrow, narrow]][mode]
    return pl.pallas_call(
        lambda *refs: shrink_kernel(rank, resident, rows, which, places, mode, *refs),
        in_specs=[smem, smem] + [vmem] * len(operands),
        out_specs=[vmem] * len(shapes),
        out_shape=shapes,
        compiler_params=pltpu.CompilerParams(vmem_limit_bytes=16 * 2**20),
        cost_estimate=pl.CostEstimate(flops=0, bytes_accessed=0, transcendentals=0),
        name="shrink_step",
    )(firsts, jnp.reshape(column, (1,)), *operands)


def expand_kernel(rank, groups, scale, count, slots_ref, slot_ref, *refs):
    parts = refs[: 2 * len(groups)]
    bases, sums, out_ref = refs[2 * len(groups) : -1 - count], refs[-1 - count : -1], refs[-1]
    shrunk = sums[0][...]
    for ref in sums[1:]:
        shrunk += ref[...]
    rows, held = out_ref.shape[0], slot_ref.shape[1]
    shrunk = jnp.transpose(jnp.concatenate([shrunk] * (held // rank), axis=0))
    slot = slot_ref[:rows]
    update = 0.0
    at = 0
    for i, depth in enumerate(groups):
        spread = jnp.concatenate(
            [
                jnp.where(slot[:, :lanes] == slots_ref[:, at + j : at + j + lanes], shrunk[:, :lanes], 0.0)
                for j in range(0, depth, held)
                for lanes in [min(held, depth - j)]
            ],
            axis=1,
        )
        at += depth
        high = spread.astype(jnp.bfloat16)
        low = (spread - high.astype(jnp.float32)).astype(jnp.bfloat16)
        for left, right in ((high, parts[2 * i]), (low, parts[2 * i]), (high, parts[2 * i + 1])):
            update += jnp.dot(left, right[...], preferred_element_type=jnp.float32)
    total = scale * update
    for base in bases:
        total += base[...]
    out_ref[...] = total.astype(jnp.bfloat16)


def expand_step(slots, slot, shrunk, parts, bases, rank, scale):
    groups = [high.shape[0] for high, _ in parts]
    flat = [term for pair in parts for term in pair]
    operands = [slots, slot, *flat, *bases, *shrunk]
    vmem = pl.BlockSpec(memory_space=pltpu.VMEM)
    return pl.pallas_call(
        lambda *refs: expand_kernel(rank, groups, scale, len(shrunk), *refs),
        in_specs=[vmem] * len(operands),
        out_specs=vmem,
        out_shape=jax.ShapeDtypeStruct(bases[0].shape, jnp.bfloat16),
        compiler_params=pltpu.CompilerParams(vmem_limit_bytes=16 * 2**20),
        cost_estimate=pl.CostEstimate(flops=0, bytes_accessed=0, transcendentals=0),
        name="expand_step",
    )(*operands)


def per_device(tokens, token_adapter_index, table, value_matrix, shrink_weight, expand_weight):
    rows, width = tokens.shape
    resident, rank, span = expand_weight.shape
    held = resident * rank
    owners = lax.axis_size("adapter")
    spots = owners // 2
    quarter = width // 4
    g, a = lax.axis_index("group"), lax.axis_index("adapter")
    c, half = a % 2, a // 2
    core_pairs = [(i, i ^ 1) for i in range(owners)]
    swap = [(0, 1), (1, 0)]
    barrier = lax.optimization_barrier

    def over_core(value):
        return lax.ppermute(value, "adapter", core_pairs)

    def over_group(value):
        return lax.ppermute(value, "group", swap)

    def shrink_rows(weight, side):
        rows_there = lax.dynamic_slice_in_dim(weight, (2 * g + side) * quarter, quarter, 0)
        return (rows_there * SHRINK_GAIN).astype(jnp.float16)

    laid = lay_out(shrink_weight, expand_weight.reshape(held, span), 2 * g + c, g, quarter)
    is_shrink = lax.broadcasted_iota(jnp.int32, laid.shape, 0) < quarter
    mine = (laid * jnp.where(is_shrink, SHRINK_GAIN, EXPAND_GAIN)).astype(jnp.float16)
    four = spots == 4
    if four:
        mine_line = FourLine(mine, half)
        mine_line.first()
    else:
        mine_line = Line(mine, spots, half)
        mine_line.advance()

    later_weight, _ = barrier((shrink_weight, mine))
    given = over_core(shrink_rows(later_weight, 1 - c))
    if four:
        given_line = FourLine(given, half)
        given_line.first()
    else:
        given_line = Line(given, spots, half)
        given_line.advance()

    later, _ = barrier((tokens, given))
    places = [2 * (1 - g) + 1 - c, 2 * (1 - g) + c, 2 * g + 1 - c]
    slot, sent, kept = pack(later, table, token_adapter_index[None, :], places, quarter)
    theirs = over_group(sent)
    came_theirs = over_core(theirs[: rows + PAD])

    source = jnp.asarray(sources(spots))[half]
    firsts = resident * (2 * source[:, None] + jnp.stack([c, 1 - c])[None, :]).reshape(-1)
    axes = ("tensor", "sub")
    two = lax.axis_size("tensor") == 2 and lax.axis_size("sub") == 1
    x = lax.axis_index("tensor")
    if four and two:
        tokens_1, mine_line.end, mine_line.middle = barrier((tokens, mine_line.end, mine_line.middle))
        mine_line.second()
        (away,) = base_product(tokens_1, value_matrix, [1 - x], span)
        given_line.end, given_line.middle, away = barrier((given_line.end, given_line.middle, away))
        given_line.second()
        tokens_2, _ = barrier((tokens, given_line.end))
        (own_base,) = base_product(tokens_2, value_matrix, [x], span)
        mine_line.far_middle, own_base = barrier((mine_line.far_middle, own_base))
        mine_line.far_end, kept = barrier((mine_line.far_end, kept))
        given_line.far_middle, away = barrier((given_line.far_middle, away))
        bases = [own_base, lax.ppermute(away, "tensor", swap)]
    elif two:
        away, own_base = base_product(tokens, value_matrix, [1 - x, x], span)
        bases = [own_base, lax.ppermute(away, "tensor", swap)]
    else:
        if four:
            mine_line.second()
            given_line.second()
        partial = jnp.dot(tokens, value_matrix, preferred_element_type=jnp.float32)
        bases = [lax.psum_scatter(partial, axes, scatter_dimension=1, tiled=True)]
    came_own = over_core(kept)

    if four:
        mine_line.third()
        given_line.third()
    else:
        for _ in range(spots - 2):
            mine_line.advance()
            given_line.advance()
    mine_pieces, given_pieces = mine_line.pieces(), given_line.pieces()

    column = (2 * g + c) * quarter

    def weights_of(start, stop):
        weights = []
        for i in range(start, stop):
            weights += [side_by_side(mine_pieces[i][:quarter]), side_by_side(given_pieces[i])]
        return weights

    def products(operands, places, weights, start, sums=(), slots=(), mode=0):
        which = list(range(start, start + len(weights)))
        return shrink_step(
            operands, places, weights, firsts, column, which, sums, slots, mode, rows, rank, resident
        )

    here_parts = ((tokens, slot, came_own), ((0, 0, 1), (2, 0, None)))
    there_parts = ((theirs, came_theirs), ((0, rows + PAD, None), (1, 0, None)))
    all_parts = (
        (tokens, slot, came_own, theirs, came_theirs),
        ((0, 0, 1), (2, 0, None), (3, rows + PAD, None), (4, 0, None)),
    )
    last = len(mine_pieces) - 1
    some = min(3, last)
    here_sum, here_slot = products(*here_parts, weights_of(0, some), 0)
    there_sum, there_slot = products(*there_parts, weights_of(0, some), 0)
    late_mine, late_given = mine_pieces, given_pieces
    if four:
        mine_line.last, here_sum = barrier((mine_line.last, here_sum))
        mine_pieces = mine_line.pieces()
        mine_line.last, given_line.last, here_sum, there_sum = barrier(
            (mine_line.last, given_line.last, here_sum, there_sum)
        )
        late_mine, late_given = mine_line.pieces(), given_line.pieces()
    sums, slots_of = (here_sum, there_sum), (here_slot, there_slot)
    for start in range(some, last, 3):
        weights = weights_of(start, min(start + 3, last))
        sums = products(*all_parts, weights, 2 * start, sums, slots_of, 1)
    weights = [side_by_side(late_mine[last][:quarter]), side_by_side(late_given[last])]
    stays, leaves = products(*all_parts, weights, 2 * last, sums, slots_of, 2)
    both_sum = stays + over_core(leaves)
    own_sum, other_sum = both_sum[:, :rows], both_sum[:, rows:]
    if len(bases) == 2:
        across = [(i, 3 - i) for i in range(4)]
        shrunk = [
            own_sum,
            lax.ppermute(other_sum, ("group", "tensor"), across),
            over_group(other_sum),
            lax.ppermute(own_sum, "tensor", swap),
        ]
    else:
        shrunk = [lax.psum(own_sum + over_group(other_sum), axes)]

    def expand_of(piece):
        cut = piece[quarter:].reshape(span // LANES, held // 2, LANES)
        return jnp.concatenate([cut[i] for i in range(span // LANES)], axis=1)

    here = jnp.concatenate([expand_of(piece) for piece in mine_pieces], axis=0)
    across, _ = barrier((over_group(here), both_sum))
    beside = over_core(jnp.concatenate([here, across], axis=0))
    terms = [two_terms(here), two_terms(across), two_terms(beside)]
    steps = jnp.arange(resident // 2, dtype=jnp.int32)
    sides = jnp.stack([c, 1 - c])[:, None, None, None]
    halves = jnp.stack([g, 1 - g])[None, :, None, None] * (resident // 2)
    slots = (2 * source[:, None] + sides) * resident + halves + steps
    slots = jnp.repeat(slots.astype(jnp.int32).reshape(1, -1), rank, axis=1)
    scale = SCALING / (SHRINK_GAIN * EXPAND_GAIN)
    return expand_step(slots, here_slot, shrunk, terms, bases, rank, scale)


def solution(mesh):
    placed = (
        P(("group", "adapter"), ("tensor", "sub")),
        P(("group", "adapter")),
        P("group"),
        P(("tensor", "sub"), None),
        P(("tensor", "sub"), "adapter"),
        P("adapter", None, ("tensor", "sub")),
    )
    return jax.shard_map(
        per_device,
        mesh=mesh,
        in_specs=placed,
        out_specs=P(("group", "adapter"), ("tensor", "sub")),
        check_vma=False,
    )
```

```python
import jax
import jax.numpy as jnp
import numpy as np
from jax import lax
from jax.experimental import pallas as pl
from jax.experimental.pallas import tpu as pltpu
from jax.sharding import PartitionSpec as P

SCALING = 0.5
SHRINK_GAIN = 2.0**19
EXPAND_GAIN = 2.0**14
LANES = 128


def sources(spots):
    if spots == 4:
        return np.array([[0, 1, 2, 3], [1, 0, 2, 3], [2, 3, 1, 0], [3, 2, 1, 0]], np.int32)
    table = []
    for half in range(spots):
        found = [half]
        for step in range(1, spots):
            up, down = half - step, half + step
            if 2 * step > spots - 1:
                found.append(up if half >= step else down)
            else:
                found += [up, down]
        table.append([f if 0 <= f < spots else -(2**16) for f in found])
    return np.array(table, np.int32)


class FourLine:
    def __init__(self, piece, half):
        self.own, self.half = piece, half

    def send(self, value, moves):
        return lax.ppermute(value, "adapter", [(2 * s + c, 2 * d + c) for s, d in moves for c in range(2)])

    def first(self):
        self.end = self.send(self.own, [(0, 1), (1, 0), (2, 3), (3, 2)])
        self.middle = self.send(self.own, [(1, 2), (2, 1)])

    def second(self):
        self.far_middle = self.send(self.end, [(1, 2), (2, 1)])
        self.far_end = self.send(self.middle, [(1, 0), (2, 3)])

    def third(self):
        self.last = self.send(self.far_middle, [(1, 0), (2, 3)])

    def pieces(self):
        inner = (self.half == 1) | (self.half == 2)
        return [
            self.own,
            self.end,
            jnp.where(inner, self.middle, self.far_end),
            jnp.where(inner, self.far_middle, self.last),
        ]


class Line:
    def __init__(self, piece, spots, half):
        self.spots, self.half = spots, half
        self.up = self.down = piece
        self.found, self.step = [piece], 1

    def send(self, value, moves):
        return lax.ppermute(value, "adapter", [(2 * s + c, 2 * d + c) for s, d in moves for c in range(2)])

    def advance(self):
        spots, step, half = self.spots, self.step, self.half
        goes_up = [(s, s + 1) for s in range(step - 1, spots - 1)]
        goes_down = [(s, s - 1) for s in range(1, spots - step + 1)]
        self.step += 1
        if 2 * step - 1 > spots:
            self.up = self.down = self.send(self.up, goes_up + goes_down)
            self.found.append(self.up)
            return
        self.up, self.down = self.send(self.up, goes_up), self.send(self.down, goes_down)
        if 2 * step > spots - 1:
            self.up = self.down = jnp.where(half >= step, self.up, self.down)
            self.found.append(self.up)
        else:
            self.found += [self.up, self.down]

    def pieces(self):
        return self.found


def two_terms(value):
    wide = value.astype(jnp.float32)
    high = lax.reduce_precision(wide, exponent_bits=8, mantissa_bits=7)
    return high.astype(jnp.bfloat16), (wide - high).astype(jnp.bfloat16)


def side_by_side(value):
    return jnp.concatenate(two_terms(value), axis=1)


def product_kernel(span, pieces, place_ref, tokens_ref, matrix_ref, *refs):
    out_refs, (tokens_here, matrix_here, token_sems, matrix_sems) = refs[:-4], refs[-4:]
    depth = tokens_ref.shape[1] // pieces
    parts = [pl.ds(k * depth, depth) for k in range(pieces)]
    copies = [[] for _ in out_refs]
    for i in range(len(out_refs)):
        columns = pl.ds(pl.multiple_of(place_ref[i] * span, LANES), span)
        for k, part in enumerate(parts):
            arriving = []
            if i == 0:
                arriving.append(
                    pltpu.make_async_copy(
                        tokens_ref.at[:, part], tokens_here.at[:, part], token_sems.at[k]
                    )
                )
            arriving.append(
                pltpu.make_async_copy(
                    matrix_ref.at[part, columns], matrix_here.at[i, part], matrix_sems.at[i, k]
                )
            )
            for copy in arriving:
                copy.start()
            copies[i].append(arriving)
    for i, out_ref in enumerate(out_refs):
        total = 0.0
        for k, part in enumerate(parts):
            for copy in copies[i][k]:
                copy.wait()
            total += jnp.dot(
                tokens_here[:, part], matrix_here[i, part], preferred_element_type=jnp.float32
            )
        out_ref[...] = total


def base_product(tokens, matrix, places, span):
    rows, width = tokens.shape
    pieces = 4
    vmem, hbm = pl.BlockSpec(memory_space=pltpu.VMEM), pl.BlockSpec(memory_space=pltpu.HBM)
    return pl.pallas_call(
        lambda *refs: product_kernel(span, pieces, *refs),
        in_specs=[pl.BlockSpec(memory_space=pltpu.SMEM), hbm, hbm],
        out_specs=[vmem] * len(places),
        out_shape=[jax.ShapeDtypeStruct((rows, span), jnp.float32)] * len(places),
        scratch_shapes=[
            pltpu.VMEM((rows, width), tokens.dtype),
            pltpu.VMEM((len(places), width, span), matrix.dtype),
            pltpu.SemaphoreType.DMA((pieces,)),
            pltpu.SemaphoreType.DMA((len(places), pieces)),
        ],
        compiler_params=pltpu.CompilerParams(vmem_limit_bytes=52 * 2**20),
        cost_estimate=pl.CostEstimate(flops=0, bytes_accessed=0, transcendentals=0),
        name="base_product",
    )(jnp.stack(places), tokens, matrix)


def lay_out_kernel(shrink_at_ref, expand_at_ref, shrink_ref, expand_ref, out_ref, sems):
    count = expand_ref.shape[0] // 2
    blocks = expand_ref.shape[1] // LANES
    quarter = out_ref.shape[0] - blocks * count
    rows = pl.ds(pl.multiple_of(shrink_at_ref[0] * quarter, 8), quarter)
    copies = [pltpu.make_async_copy(shrink_ref.at[rows], out_ref.at[pl.ds(0, quarter)], sems.at[0])]
    held = pl.ds(pl.multiple_of(expand_at_ref[0] * count, 8), count)
    for i in range(blocks):
        copies.append(
            pltpu.make_async_copy(
                expand_ref.at[held, pl.ds(i * LANES, LANES)],
                out_ref.at[pl.ds(quarter + i * count, count)],
                sems.at[i + 1],
            )
        )
    for copy in copies:
        copy.start()
    for copy in copies:
        copy.wait()


def lay_out(shrink, expand, shrink_at, expand_at, quarter):
    held, span = expand.shape
    smem, hbm = pl.BlockSpec(memory_space=pltpu.SMEM), pl.BlockSpec(memory_space=pltpu.HBM)
    rows = quarter + held // 2 * (span // LANES)
    return pl.pallas_call(
        lay_out_kernel,
        in_specs=[smem, smem, hbm, hbm],
        out_specs=pl.BlockSpec(memory_space=pltpu.VMEM),
        out_shape=jax.ShapeDtypeStruct((rows, LANES), jnp.float32),
        scratch_shapes=[pltpu.SemaphoreType.DMA((span // LANES + 1,))],
        compiler_params=pltpu.CompilerParams(vmem_limit_bytes=16 * 2**20),
        cost_estimate=pl.CostEstimate(flops=0, bytes_accessed=0, transcendentals=0),
        name="lay_out",
    )(jnp.reshape(shrink_at, (1,)), jnp.reshape(expand_at, (1,)), shrink, expand)


PAD = 16


def pack_kernel(rows, quarter, *refs):
    column_refs, (table_ref, index_ref, tokens_ref, slot_ref, sent_ref, kept_ref, sems) = refs[:3], refs[3:]
    step = rows + PAD
    places = ((sent_ref, 0), (sent_ref, step), (kept_ref, 0))
    copies = []
    for i, (out_ref, start) in enumerate(places):
        column = pl.multiple_of(column_refs[i][0] * quarter, LANES)
        copies.append(
            pltpu.make_async_copy(
                tokens_ref.at[:, pl.ds(column, quarter)], out_ref.at[pl.ds(start, rows)], sems.at[i]
            )
        )
        copies[i].start()
    index = index_ref[...]
    slot = jnp.zeros_like(index)
    for j in range(table_ref.shape[0]):
        slot += jnp.where(index == j, table_ref[j], 0)
    slot_ref[...] = slot
    tail = jnp.broadcast_to(slot.astype(jnp.float32), (PAD, rows)).astype(sent_ref.dtype)
    for out_ref, start in places:
        out_ref[start + rows : start + step, :rows] = tail
        if quarter > rows:
            out_ref[start + rows : start + step, rows:] = jnp.zeros((PAD, quarter - rows), out_ref.dtype)
    for copy in copies:
        copy.wait()


def pack(tokens, table, index, places, quarter):
    rows = tokens.shape[0]
    vmem, smem = pl.BlockSpec(memory_space=pltpu.VMEM), pl.BlockSpec(memory_space=pltpu.SMEM)
    return pl.pallas_call(
        lambda *refs: pack_kernel(rows, quarter, *refs),
        in_specs=[smem] * 4 + [vmem, pl.BlockSpec(memory_space=pltpu.HBM)],
        out_specs=[vmem] * 3,
        out_shape=[
            jax.ShapeDtypeStruct((1, rows), jnp.int32),
            jax.ShapeDtypeStruct((2 * (rows + PAD), quarter), tokens.dtype),
            jax.ShapeDtypeStruct((rows + PAD, quarter), tokens.dtype),
        ],
        scratch_shapes=[pltpu.SemaphoreType.DMA((3,))],
        compiler_params=pltpu.CompilerParams(vmem_limit_bytes=16 * 2**20),
        cost_estimate=pl.CostEstimate(flops=0, bytes_accessed=0, transcendentals=0),
        name="pack",
    )(*[jnp.reshape(place, (1,)) for place in places], table, index, tokens)


def flip(value, by):
    return 1 - value if by else value


def first_slot(source_ref, spot, piece, core, resident):
    return resident * (2 * source_ref[spot, piece] + core)


def shrink_kernel(rank, resident, rows, which, places, mode, source_ref, spot_ref, core_ref, column_ref, *refs):
    held = rank * resident
    count = 1 + max(max(p[0], p[2] or 0) for p in places)
    operands, refs = refs[:count], refs[count:]
    weights, refs = refs[: len(which)], refs[len(which) :]
    quarter = weights[0].shape[0]
    group = lax.broadcasted_iota(jnp.int32, (1, held), 1) // rank

    def rows_of(arrays, part):
        per = arrays[0].shape[0] // rows
        return arrays[part // per][part % per * rows : (part % per + 1) * rows]

    if mode:
        outs = refs[-mode:]
        inputs = refs[:-mode]
        slot_rows = inputs[-(len(places) // 2) :]
        sums = inputs[: -(len(places) // 2)]
    for part, (operand, row, slots) in enumerate(places):
        if slots is None:
            tokens = operands[operand][row : row + rows]
        else:
            tokens = operands[operand][:, pl.ds(pl.multiple_of(column_ref[0], quarter), quarter)]
        if mode:
            slot = rows_of(slot_rows, part)
            total = rows_of(sums, part)
        else:
            if slots is None:
                slot = operands[operand][row + rows : row + rows + PAD, :rows].astype(jnp.float32)[:1]
            else:
                slot = operands[slots][...].astype(jnp.float32)
            slot = jnp.transpose(jnp.broadcast_to(slot, (held, rows))).astype(jnp.int32)
            refs[1][part * rows : (part + 1) * rows] = slot
            total = jnp.zeros((rows, held), jnp.float32)
        for w, side in zip(weights, which):
            product = jnp.dot(tokens, w[...], preferred_element_type=jnp.float32)
            first = first_slot(source_ref, spot_ref[0], side // 2, flip(core_ref[0], side % 2), resident)
            chosen = slot == first + group
            total = jnp.where(chosen, product[:, :held] + product[:, held:], total)
        if mode < 2:
            out_ref = outs[0] if mode else refs[0]
            out_ref[part * rows : (part + 1) * rows] = total
        else:
            total = jnp.transpose(total)
            gathered = total[:rank]
            for j in range(1, resident):
                gathered += total[j * rank : (j + 1) * rank]
            at = part // 2 * rows
            outs[part % 2][:, at : at + rows] = gathered


def shrink_step(operands, places, weights, facts, which, sums, slots, mode, rows, rank, resident):
    vmem = pl.BlockSpec(memory_space=pltpu.VMEM)
    smem = pl.BlockSpec(memory_space=pltpu.SMEM)
    operands = [*operands, *weights, *sums, *slots]
    count, held = len(places) * rows, rank * resident
    wide = jax.ShapeDtypeStruct((count, held), jnp.float32)
    narrow = jax.ShapeDtypeStruct((rank, count // 2), jnp.float32)
    shapes = [[wide, jax.ShapeDtypeStruct((count, held), jnp.int32)], [wide], [narrow, narrow]][mode]
    return pl.pallas_call(
        lambda *refs: shrink_kernel(rank, resident, rows, which, places, mode, *refs),
        in_specs=[smem] * 4 + [vmem] * len(operands),
        out_specs=[vmem] * len(shapes),
        out_shape=shapes,
        compiler_params=pltpu.CompilerParams(vmem_limit_bytes=16 * 2**20),
        cost_estimate=pl.CostEstimate(flops=0, bytes_accessed=0, transcendentals=0),
        name="shrink_step",
    )(*facts[:3], facts[4], *operands)


def expand_kernel(rank, groups, scale, count, slots_ref, slot_ref, *refs):
    parts = refs[: 2 * len(groups)]
    bases, sums, out_ref = refs[2 * len(groups) : -1 - count], refs[-1 - count : -1], refs[-1]
    shrunk = sums[0][...]
    for ref in sums[1:]:
        shrunk += ref[...]
    rows, held = out_ref.shape[0], slot_ref.shape[1]
    shrunk = jnp.transpose(jnp.concatenate([shrunk] * (held // rank), axis=0))
    slot = slot_ref[:rows]
    update = 0.0
    at = 0
    for i, depth in enumerate(groups):
        spread = jnp.concatenate(
            [
                jnp.where(slot[:, :lanes] == slots_ref[:, at + j : at + j + lanes], shrunk[:, :lanes], 0.0)
                for j in range(0, depth, held)
                for lanes in [min(held, depth - j)]
            ],
            axis=1,
        )
        at += depth
        high = spread.astype(jnp.bfloat16)
        low = (spread - high.astype(jnp.float32)).astype(jnp.bfloat16)
        for left, right in ((high, parts[2 * i]), (low, parts[2 * i]), (high, parts[2 * i + 1])):
            update += jnp.dot(left, right[...], preferred_element_type=jnp.float32)
    total = scale * update
    for base in bases:
        total += base[...]
    out_ref[...] = total.astype(jnp.bfloat16)


def expand_step(slots, slot, shrunk, parts, bases, rank, scale):
    groups = [high.shape[0] for high, _ in parts]
    flat = [term for pair in parts for term in pair]
    operands = [slots, slot, *flat, *bases, *shrunk]
    vmem = pl.BlockSpec(memory_space=pltpu.VMEM)
    return pl.pallas_call(
        lambda *refs: expand_kernel(rank, groups, scale, len(shrunk), *refs),
        in_specs=[vmem] * len(operands),
        out_specs=vmem,
        out_shape=jax.ShapeDtypeStruct(bases[0].shape, jnp.bfloat16),
        compiler_params=pltpu.CompilerParams(vmem_limit_bytes=16 * 2**20),
        cost_estimate=pl.CostEstimate(flops=0, bytes_accessed=0, transcendentals=0),
        name="expand_step",
    )(*operands)


def per_device(tokens, token_adapter_index, table, value_matrix, shrink_weight, expand_weight):
    rows, width = tokens.shape
    resident, rank, span = expand_weight.shape
    held = resident * rank
    owners = lax.axis_size("adapter")
    spots = owners // 2
    quarter = width // 4
    g, a = lax.axis_index("group"), lax.axis_index("adapter")
    c, half = a % 2, a // 2
    core_pairs = [(i, i ^ 1) for i in range(owners)]
    swap = [(0, 1), (1, 0)]
    barrier = lax.optimization_barrier

    def over_core(value):
        return lax.ppermute(value, "adapter", core_pairs)

    def over_group(value):
        return lax.ppermute(value, "group", swap)

    def shrink_rows(weight, side):
        rows_there = lax.dynamic_slice_in_dim(weight, (2 * g + side) * quarter, quarter, 0)
        return (rows_there * SHRINK_GAIN).astype(jnp.float16)

    laid = lay_out(shrink_weight, expand_weight.reshape(held, span), 2 * g + c, g, quarter)
    is_shrink = lax.broadcasted_iota(jnp.int32, laid.shape, 0) < quarter
    mine = (laid * jnp.where(is_shrink, SHRINK_GAIN, EXPAND_GAIN)).astype(jnp.float16)
    four = spots == 4
    if four:
        mine_line = FourLine(mine, half)
        mine_line.first()
    else:
        mine_line = Line(mine, spots, half)
        mine_line.advance()

    later_weight, _ = barrier((shrink_weight, mine))
    given = over_core(shrink_rows(later_weight, 1 - c))
    if four:
        given_line = FourLine(given, half)
        given_line.first()
    else:
        given_line = Line(given, spots, half)
        given_line.advance()

    later, _ = barrier((tokens, given))
    places = [2 * (1 - g) + 1 - c, 2 * (1 - g) + c, 2 * g + 1 - c]
    slot, sent, kept = pack(later, table, token_adapter_index[None, :], places, quarter)
    theirs = over_group(sent)
    came_theirs = over_core(theirs[: rows + PAD])

    axes = ("tensor", "sub")
    two = lax.axis_size("tensor") == 2 and lax.axis_size("sub") == 1
    x = lax.axis_index("tensor")
    if four and two:
        tokens_1, mine_line.end, mine_line.middle = barrier((tokens, mine_line.end, mine_line.middle))
        mine_line.second()
        (away,) = base_product(tokens_1, value_matrix, [1 - x], span)
        given_line.end, given_line.middle, away = barrier((given_line.end, given_line.middle, away))
        given_line.second()
        tokens_2, _ = barrier((tokens, given_line.end))
        (own_base,) = base_product(tokens_2, value_matrix, [x], span)
        mine_line.far_middle, own_base = barrier((mine_line.far_middle, own_base))
        mine_line.far_end, kept = barrier((mine_line.far_end, kept))
        given_line.far_middle, away = barrier((given_line.far_middle, away))
        bases = [own_base, lax.ppermute(away, "tensor", swap)]
    elif two:
        away, own_base = base_product(tokens, value_matrix, [1 - x, x], span)
        bases = [own_base, lax.ppermute(away, "tensor", swap)]
    else:
        if four:
            mine_line.second()
            given_line.second()
        partial = jnp.dot(tokens, value_matrix, preferred_element_type=jnp.float32)
        bases = [lax.psum_scatter(partial, axes, scatter_dimension=1, tiled=True)]
    came_own = over_core(kept)

    if four:
        mine_line.third()
        given_line.third()
    else:
        for _ in range(spots - 2):
            mine_line.advance()
            given_line.advance()
    mine_pieces, given_pieces = mine_line.pieces(), given_line.pieces()

    scalars = (half, c, g, (2 * g + c) * quarter)
    facts = [jnp.asarray(sources(spots))] + [jnp.reshape(value, (1,)) for value in scalars]

    def weights_of(start, stop):
        weights = []
        for i in range(start, stop):
            weights += [side_by_side(mine_pieces[i][:quarter]), side_by_side(given_pieces[i])]
        return weights

    def products(operands, places, weights, start, sums=(), slots=(), mode=0):
        which = list(range(start, start + len(weights)))
        return shrink_step(
            operands, places, weights, facts, which, sums, slots, mode, rows, rank, resident
        )

    here_parts = ((tokens, slot, came_own), ((0, 0, 1), (2, 0, None)))
    there_parts = ((theirs, came_theirs), ((0, rows + PAD, None), (1, 0, None)))
    all_parts = (
        (tokens, slot, came_own, theirs, came_theirs),
        ((0, 0, 1), (2, 0, None), (3, rows + PAD, None), (4, 0, None)),
    )
    last = len(mine_pieces) - 1
    some = min(3, last)
    here_sum, here_slot = products(*here_parts, weights_of(0, some), 0)
    there_sum, there_slot = products(*there_parts, weights_of(0, some), 0)
    late_mine, late_given = mine_pieces, given_pieces
    if four:
        mine_line.last, here_sum = barrier((mine_line.last, here_sum))
        mine_pieces = mine_line.pieces()
        mine_line.last, given_line.last, here_sum, there_sum = barrier(
            (mine_line.last, given_line.last, here_sum, there_sum)
        )
        late_mine, late_given = mine_line.pieces(), given_line.pieces()
    sums, slots_of = (here_sum, there_sum), (here_slot, there_slot)
    for start in range(some, last, 3):
        weights = weights_of(start, min(start + 3, last))
        sums = products(*all_parts, weights, 2 * start, sums, slots_of, 1)
    weights = [side_by_side(late_mine[last][:quarter]), side_by_side(late_given[last])]
    stays, leaves = products(*all_parts, weights, 2 * last, sums, slots_of, 2)
    both_sum = stays + over_core(leaves)
    own_sum, other_sum = both_sum[:, :rows], both_sum[:, rows:]
    if len(bases) == 2:
        across = [(i, 3 - i) for i in range(4)]
        shrunk = [
            own_sum,
            lax.ppermute(other_sum, ("group", "tensor"), across),
            over_group(other_sum),
            lax.ppermute(own_sum, "tensor", swap),
        ]
    else:
        shrunk = [lax.psum(own_sum + over_group(other_sum), axes)]

    def expand_of(piece):
        cut = piece[quarter:].reshape(span // LANES, held // 2, LANES)
        return jnp.concatenate([cut[i] for i in range(span // LANES)], axis=1)

    here = jnp.concatenate([expand_of(piece) for piece in mine_pieces], axis=0)
    across, _ = barrier((over_group(here), both_sum))
    beside = over_core(jnp.concatenate([here, across], axis=0))
    terms = [two_terms(here), two_terms(across), two_terms(beside)]
    late_half = half
    source = jnp.asarray(sources(spots))[late_half]
    steps = jnp.arange(resident // 2, dtype=jnp.int32)
    sides = jnp.stack([c, 1 - c])[:, None, None, None]
    halves = jnp.stack([g, 1 - g])[None, :, None, None] * (resident // 2)
    slots = (2 * source[:, None] + sides) * resident + halves + steps
    slots = jnp.repeat(slots.astype(jnp.int32).reshape(1, -1), rank, axis=1)
    scale = SCALING / (SHRINK_GAIN * EXPAND_GAIN)
    return expand_step(slots, here_slot, shrunk, terms, bases, rank, scale)


def solution(mesh):
    placed = (
        P(("group", "adapter"), ("tensor", "sub")),
        P(("group", "adapter")),
        P("group"),
        P(("tensor", "sub"), None),
        P(("tensor", "sub"), "adapter"),
        P("adapter", None, ("tensor", "sub")),
    )
    return jax.shard_map(
        per_device,
        mesh=mesh,
        in_specs=placed,
        out_specs=P(("group", "adapter"), ("tensor", "sub")),
        check_vma=False,
    )
```
